512 devices in a mesh: dp: 8 (over y), fsdp: 8 (over x, z_lo), tensor: 8 (over z_hi, core).
Axes of the slice: x: 4, y: 8, z: 8 (z_hi: 4, z_lo: 2; z = z_hi * 2 + z_lo), core: 2. Of those that a mesh axis runs over, the one named last changes fastest.
Arguments:
- teacher_in: bfloat16 [16384, 4096], P(('dp', 'fsdp'), 'tensor'), may hold values from -6 to 6
- codes: int32 [4096, 1024], P('tensor'), may hold values from 0 to 65535
- scales: bfloat16 [32, 4096], P('tensor'), may hold values from 0.0019989014 to 0.0079956055
- teacher_resid: bfloat16 [16384, 8, 512], P(('dp', 'fsdp'), None, 'tensor'), may hold values from -48 to 48
- teacher_gain: bfloat16 [8, 512], P(None, 'tensor'), may hold values from 0.5 to 1.5
- projector: bfloat16 [8, 512, 1792], P('fsdp', 'tensor'), may hold values from -0.09375 to 0.09375
- routes: int32 [2048, 1], replicated, may hold values from 0 to 7; in each aligned block of 4 rows (0 to 3, 4 to 7, ...) no two rows name the same one
- student_in: bfloat16 [131072, 1792], P(('dp', 'fsdp', 'tensor')), may hold values from -6 to 6
- queries: bfloat16 [131072, 1792], P(('dp', 'fsdp', 'tensor')), may hold values from -6 to 6
- keys: bfloat16 [131072, 256], P(('dp', 'fsdp', 'tensor')), may hold values from -6 to 6
- segments: int32 [131072], P(('dp', 'fsdp', 'tensor')), may hold values from 0 to 8191, never falling along the last dimension, each value on 1 to 128 neighbouring positions
- value_weight: bfloat16 [1792, 256], P(('fsdp', 'tensor')), may hold values from -0.125 to 0.125
Outputs:
- loss: float32 [], replicated
- grad_value: float32 [1792, 256], P(('fsdp', 'tensor'))
The draws below stay inside these ranges and needn't reach their ends.
Inputs may be any that keep to these rules, and one draw needn't show every extreme that they name: `routes`: each row names the student data group of one teacher block of 8 rows; the 4 blocks of one device go to different groups. `segments`: document ids never fall along the rows; each document has at most 128 tokens.
All inputs are finite; a program needn't handle non-finite values.
Results may differ from the reference program's by a relative error of at most 0.0055.
Values may be sent and summed in bfloat16 or wider, within the bound.
A program may use at most 64 MiB of HBM per device.

```python
import math
import jax
import jax.numpy as jnp
import numpy as np
from jax import lax

HT_IN = 4096
HT = 4096
GROUP = 128
QH = 14
KH = 2
HEAD = 128
DS = 1792
BLK = 8
NB_DEV = 4
S_DEV = 256
TT = 256
TT_ALL = 16384
S_ALL = 131072
NBLK_ALL = 2048
QW = 1792
KVW = 256
N_DP = 8
N_FSDP = 8
N_TENSOR = 8


def planted_rows(key):
    stride = max(8, S_DEV // 8)
    rows = jnp.arange(S_ALL, dtype=jnp.int32)
    offset = rows % S_DEV % stride
    self_row = offset == stride // 2
    prior_row = offset == stride // 2 - 1
    pair_count = S_ALL // stride
    levels = jax.random.randint(jax.random.fold_in(key, 101), (pair_count,), 3, 7).astype(jnp.float32)
    flips = jax.random.bernoulli(jax.random.fold_in(key, 102), 0.5, (pair_count, HEAD))
    pattern = jnp.where(flips, 1.0, -1.0).astype(jnp.float32)
    pair = rows // stride
    return (self_row, prior_row, levels[pair], pattern[pair])


def draw_queries(key, part):
    self_row, prior_row, strength, pattern = planted_rows(key)
    key = jax.random.fold_in(key, 7)
    noise = jnp.clip(jax.random.normal(jax.random.fold_in(key, 2), (S_ALL, QH, HEAD)), -6.0, 6.0)
    aligned = (strength[:, None] * pattern)[:, None, :]
    result = jnp.where(self_row[:, None, None], aligned, noise)
    return result.reshape(S_ALL, QH * HEAD).astype(jnp.bfloat16)


def draw_keys(key, part):
    self_row, prior_row, strength, pattern = planted_rows(key)
    key = jax.random.fold_in(key, 8)
    noise = jnp.clip(jax.random.normal(jax.random.fold_in(key, 2), (S_ALL, KH, HEAD)), -6.0, 6.0)
    aligned = (strength[:, None] * pattern)[:, None, :]
    nearby = ((strength[:, None] - 0.03125) * pattern)[:, None, :]
    result = jnp.where(self_row[:, None, None], aligned, jnp.where(prior_row[:, None, None], nearby, noise))
    return result.reshape(S_ALL, KH * HEAD).astype(jnp.bfloat16)


def draw_teacher_resid(key, part):
    key = jax.random.fold_in(key, 9)
    width = HT // N_FSDP
    slab = HT // (N_FSDP * N_TENSOR)
    column = jnp.arange(width, dtype=jnp.int32)
    owner = (column // slab).astype(jnp.float32)
    rising = 0.8 * jnp.exp(owner * (math.log(4.0) / max(1, N_TENSOR - 1)))
    jitter = jnp.exp(jax.random.uniform(jax.random.fold_in(key, 1), (N_FSDP, width), minval=0.0, maxval=math.log(2.0)))
    column_scale = (rising[None, :] * jitter)[None]
    row_scale = jnp.exp(jax.random.uniform(jax.random.fold_in(key, 2), (TT_ALL, 1, 1), minval=0.0, maxval=math.log(3.0)))
    noise = jnp.clip(jax.random.normal(jax.random.fold_in(key, 3), (TT_ALL, N_FSDP, width)), -3.0, 3.0)
    result = jnp.clip(noise * row_scale * column_scale, -48.0, 48.0)
    return result.astype(jnp.bfloat16)


def with_ends(drawn, own_key, low, largest):
    index_at = [jax.random.randint(jax.random.fold_in(own_key, axis), (), 0, length) for axis, length in enumerate(drawn.shape)]
    longest = drawn.shape.index(max(drawn.shape))
    neighbour = index_at[:longest] + [(index_at[longest] + 1) % drawn.shape[longest]] + index_at[longest + 1:]
    return drawn.at[tuple(index_at)].set(low).at[tuple(neighbour)].set(largest)


def shard_levels(own_key, dims, shards, smallest, largest):
    level = 1.0
    for position, blocks in shards:
        heights = jax.random.uniform(jax.random.fold_in(jax.random.fold_in(own_key, 6), position), (blocks,), jnp.float32, smallest / len(shards), largest / len(shards))
        level = level * jnp.repeat(jnp.exp(heights), dims[position] // blocks).reshape((-1,) + (1,) * (len(dims) - 1 - position))
    return level


def profile(amount, total, limit, skew):
    loads = [(1 << 20) // math.isqrt(rank ** skew) + 1 for rank in range(2, amount + 1)]
    spare, holding = total - limit - (amount - 1), [1] * (amount - 1)
    while spare > 0:
        candidates = [i for i in range(amount - 1) if holding[i] < limit]
        pool, remaining = sum([loads[i] for i in candidates]), spare
        for i in candidates:
            addition = min(limit - holding[i], max(1, remaining * loads[i] // pool), spare)
            holding[i] = holding[i] + addition
            spare = spare - addition
    return np.array([limit] + holding)


def ragged_sizes(own_key, count, total, reach, lean):
    if count == 2:
        one = jax.random.randint(own_key, (), max(1, total - reach), min(reach, total - 1) + 1)
        return jnp.stack([one, total - one])
    sizes = jnp.asarray(profile(count, total, reach, lean), jnp.int32)
    twos = (count - 1) // 2
    giver, sink = sizes[1:1 + 2 * twos:2], sizes[2:2 + 2 * twos:2]
    room = jnp.minimum(giver - 1, reach - sink)
    shifted = jax.random.randint(jax.random.fold_in(own_key, 1), (twos,), 0, 1 << 20) % (room + 1)
    sizes = sizes.at[1:1 + 2 * twos:2].set(giver - shifted).at[2:2 + 2 * twos:2].set(sink + shifted)
    return sizes[jax.random.permutation(jax.random.fold_in(own_key, 2), count)]


def assign_block(stream_key, own, number, rows, count, top, limit, slope):
    order = jax.random.permutation(stream_key, count)
    crowded, usual = portions_of(count, rows * top, limit, slope, True), portions_of(count, rows * top, limit, slope, False)
    places = jnp.arange(count)

    def named(sizes, turn):
        used = int((sizes > 0).sum())
        fixed = max(1, used // 4)
        shifted = fixed + (places - fixed + turn * (used - fixed)) % max(1, count - fixed)
        return jnp.zeros((count,), jnp.int32).at[order[jnp.where(places < fixed, places, shifted)]].set(jnp.asarray(sizes, jnp.int32))

    sizes = jnp.where(number % 4 == 0, named(crowded, number // 4), named(usual, number - number // 4 - 1))
    mixed = jax.random.permutation(jax.random.fold_in(own, 3), count)
    giver, receiver = mixed[0:count // 2 * 2:2], mixed[1:count // 2 * 2:2]
    margin = jnp.minimum(sizes[giver] - 1, limit - sizes[receiver]) // 2
    margin = jnp.where((giver == order[0]) | (receiver == order[0]) | (sizes[receiver] == 0), 0, jnp.maximum(margin, 0))
    shifted = jax.random.randint(jax.random.fold_in(own, 4), (count // 2,), 0, 1 << 20) % (margin + 1)
    sizes = sizes.at[giver].add(-shifted).at[receiver].add(shifted)
    items = jnp.searchsorted(jnp.cumsum(sizes), jnp.arange(rows * top), side="right").astype(jnp.int32)
    grid = items.reshape(top, rows).T
    grid = grid[jax.random.permutation(jax.random.fold_in(own, 1), rows)]
    turn = jax.random.randint(jax.random.fold_in(own, 2), (rows, 1), 0, top)
    return jnp.take_along_axis(grid, (jnp.arange(top)[None, :] + turn) % top, axis=1)


def portions_of(number_of, total, reach, slope, full):
    portions = [(1 << 20) // math.isqrt(standing ** slope) + 1 for standing in range(1, number_of + 1)]
    largest = reach if full else min(reach, max(-(-total // number_of), total * portions[0] // sum(portions)))
    least = 1 if total - largest >= number_of - 1 else 0
    holding, spare = [largest] + [least] * (number_of - 1), total - largest - least * (number_of - 1)
    while spare > 0:
        candidates = [i for i in range(1, number_of) if holding[i] < largest] or [i for i in range(1, number_of) if holding[i] < reach]
        pool, budget = sum([portions[i] for i in candidates]), spare
        for i in candidates:
            more = min(reach - holding[i], max(1, budget * portions[i] // pool), spare)
            holding[i] = holding[i] + more
            spare = spare - more
    return np.array(holding)


def gaussian(own_key, dims, scale, limit, split=(), kind=jnp.bfloat16):
    array = jax.random.normal(own_key, dims, jnp.float32) * scale
    if len(split) > 0:
        array = shard_levels(own_key, dims, split, -0.22, 0.18) * array
    return jnp.clip(array, min=-limit, max=limit).astype(kind)


def setup_inputs(seed: int = 0) -> dict:
    splits = jax.random.split(jax.random.key(seed), 13)
    teacher_in = gaussian(splits[0], (TT_ALL, HT_IN), 1.0, 6.0, ((0, 64), (1, 8)))
    codes = with_ends(jax.random.randint(splits[1], (HT_IN, HT // 4), 0, 65536), jax.random.fold_in(splits[1], 1), 0, 65535).astype(jnp.int32)
    scales = jnp.clip(jnp.exp(math.log(0.0079956055) - 1.3862944 * jax.random.uniform(splits[2], (HT_IN // GROUP, HT), jnp.float32) ** shard_levels(splits[2], (HT_IN // GROUP, HT), ((0, 8),), -0.2, 0.2)), 0.0019989014, 0.0079956055).astype(jnp.bfloat16)
    teacher_resid = draw_teacher_resid(jax.random.fold_in(splits[12], 71), 0)
    teacher_gain = jnp.clip(1.0 + 0.1 * jax.random.normal(splits[4], (N_FSDP, HT // N_FSDP), jnp.float32), 0.5, 1.5).astype(jnp.bfloat16)
    projector = gaussian(splits[5], (N_FSDP, HT // N_FSDP, QW), HT ** -0.5, 0.09375, ((0, 8), (1, 8)))
    routes_keys = jax.random.split(jax.random.fold_in(splits[6], 1), NBLK_ALL // NB_DEV)
    routes_turns = jax.random.permutation(jax.random.fold_in(splits[6], 3), NBLK_ALL // NB_DEV)
    routes = jax.vmap(lambda own, number: assign_block(jax.random.fold_in(splits[6], 2), own, number, NB_DEV, N_DP, 1, 1, 2))(routes_keys, routes_turns).reshape((NBLK_ALL, 1))
    student_in = gaussian(splits[7], (S_ALL, DS), 1.0, 6.0, ((0, 512),))
    queries = draw_queries(jax.random.fold_in(splits[12], 71), 0)
    keys = draw_keys(jax.random.fold_in(splits[12], 71), 0)
    segments = jnp.searchsorted(jnp.cumsum(ragged_sizes(splits[10], S_ALL // 16, S_ALL, max(32, S_DEV // 2), 2)), jnp.arange(S_ALL), side="right").astype(jnp.int32)
    value_weight = gaussian(splits[11], (DS, KVW), DS ** -0.5, 0.125, ((0, 64),))
    return dict(teacher_in=teacher_in, codes=codes, scales=scales, teacher_resid=teacher_resid, teacher_gain=teacher_gain, projector=projector, routes=routes, student_in=student_in, queries=queries, keys=keys, segments=segments, value_weight=value_weight)


EPS = 1e-06

def unpack_levels(codes):
    pieces = [jnp.bitwise_and(jnp.right_shift(codes, 4 * shift_step), 15) for shift_step in range(4)]
    stacked = jnp.stack(pieces, axis=-1)
    return stacked.reshape(codes.shape[0], codes.shape[1] * 4)

def dequantize(codes, scales):
    levels = unpack_levels(codes).astype(jnp.float32) - 8.0
    spread = jnp.repeat(scales.astype(jnp.float32), GROUP, axis=0)
    return (levels * spread).astype(jnp.bfloat16)

def student_device(student_rows, query_rows, key_rows, segment_rows, target_rows, mask_rows, value_weight):
    count = query_rows.shape[0]
    members = QH // KH
    values = jnp.dot(student_rows, value_weight, preferred_element_type=jnp.float32).astype(jnp.bfloat16)
    query_heads = query_rows.reshape(count, KH, members, HEAD).astype(jnp.float32)
    key_heads = key_rows.reshape(count, KH, HEAD).astype(jnp.float32)
    value_heads = values.reshape(count, KH, HEAD).astype(jnp.float32)
    scores = jnp.einsum('sgkd,tgd->gkst', query_heads, key_heads) * HEAD ** (-0.5)
    places = jnp.arange(count, dtype=jnp.int32)
    allowed = (segment_rows[:, None] == segment_rows[None, :]) & (places[:, None] >= places[None, :])
    scores = jnp.where(allowed, scores, -1e+30)
    highest = lax.optimization_barrier(jnp.max(scores, axis=-1, keepdims=True))
    weights = jnp.exp(scores - highest)
    probs = (weights / lax.optimization_barrier(jnp.sum(weights, axis=-1, keepdims=True))).astype(jnp.bfloat16)
    attended = jnp.einsum('gkst,tgd->sgkd', probs.astype(jnp.float32), value_heads).reshape(count, QH * HEAD)
    diff = attended - target_rows.astype(jnp.float32)
    masked = diff * mask_rows[:, None]
    loss_term = jnp.sum(masked * diff)
    grad_att = (2.0 * masked / (QH * HEAD)).astype(jnp.bfloat16)
    grad_heads = grad_att.reshape(count, KH, members, HEAD).astype(jnp.float32)
    grad_values = jnp.einsum('gkst,sgkd->tgd', probs.astype(jnp.float32), grad_heads).reshape(count, KH * HEAD).astype(jnp.bfloat16)
    grad_weight = lax.dot_general(student_rows, grad_values, (((0,), (0,)), ((), ())), preferred_element_type=jnp.float32)
    return (loss_term, grad_weight)

def reference(teacher_in, codes, scales, teacher_resid, teacher_gain, projector, routes, student_in, queries, keys, segments, value_weight):
    query_width = QH * HEAD
    weight = dequantize(codes, scales)
    slab_rows = HT_IN // N_TENSOR
    weight_parts = weight.reshape(N_TENSOR, slab_rows, HT).astype(jnp.float32)
    group_count = N_DP * N_FSDP
    inputs = teacher_in.reshape(group_count, TT, N_TENSOR, slab_rows)
    residual = teacher_resid.reshape(group_count, TT, HT)
    gain = teacher_gain.reshape(HT).astype(jnp.float32)
    slab_cols = HT // (N_FSDP * N_TENSOR)
    proj = projector.reshape(N_FSDP, N_TENSOR, slab_cols, query_width).astype(jnp.float32)

    def teacher_group(pair):
        rows_in, rows_res = pair
        parts = jnp.einsum('rtk,tkc->trc', rows_in.astype(jnp.float32), weight_parts)
        rounded = lax.optimization_barrier(parts.astype(jnp.bfloat16)).astype(jnp.float32)
        hidden = lax.optimization_barrier(jnp.sum(rounded, axis=0)) + rows_res.astype(jnp.float32)
        mean_square = lax.optimization_barrier(jnp.mean(hidden * hidden, axis=1, keepdims=True))
        normed = (hidden * lax.rsqrt(mean_square + EPS) * gain).astype(jnp.bfloat16)
        shaped = normed.reshape(TT, N_FSDP, N_TENSOR, slab_cols).astype(jnp.float32)
        tparts = jnp.einsum('rftc,ftcq->trq', shaped, proj)
        trounded = lax.optimization_barrier(tparts.astype(jnp.bfloat16)).astype(jnp.float32)
        return lax.optimization_barrier(jnp.sum(trounded, axis=0)).astype(jnp.bfloat16)
    targets = lax.map(teacher_group, (inputs, residual))
    per_group = TT // BLK
    block_total = group_count * per_group
    blocks = targets.reshape(block_total, BLK, query_width)
    index = jnp.arange(block_total, dtype=jnp.int32)
    src_dp = index // (N_FSDP * per_group)
    src_fsdp = index // per_group % N_FSDP
    src_tensor = index // NB_DEV % N_TENSOR
    dest = routes[:, 0]
    placed = jnp.zeros((N_DP, N_FSDP, N_TENSOR, N_DP, BLK, query_width), jnp.bfloat16)
    placed = placed.at[dest, src_fsdp, src_tensor, src_dp].set(blocks)
    marks = jnp.zeros((N_DP, N_FSDP, N_TENSOR, N_DP), jnp.float32)
    marks = marks.at[dest, src_fsdp, src_tensor, src_dp].set(1.0)
    device_count = N_DP * N_FSDP * N_TENSOR
    lead_rows = N_DP * BLK
    extra = S_DEV - lead_rows
    student_target = jnp.concatenate([placed.reshape(device_count, lead_rows, query_width), jnp.zeros((device_count, extra, query_width), jnp.bfloat16)], axis=1)
    row_mask = jnp.concatenate([jnp.repeat(marks.reshape(device_count, N_DP), BLK, axis=1), jnp.zeros((device_count, extra), jnp.float32)], axis=1)
    stacked = (student_in.reshape(device_count, S_DEV, DS), queries.reshape(device_count, S_DEV, query_width), keys.reshape(device_count, S_DEV, KH * HEAD), segments.reshape(device_count, S_DEV), student_target, row_mask)

    def step(carry, item):
        loss_term, grad_weight = student_device(item[0], item[1], item[2], item[3], item[4], item[5], value_weight)
        return ((carry[0] + loss_term, carry[1] + grad_weight), None)
    start = (jnp.zeros((), jnp.float32), jnp.zeros((DS, KH * HEAD), jnp.float32))
    totals, unused = lax.scan(step, start, stacked)
    loss = totals[0] / (TT * N_DP * N_FSDP * query_width)
    return (loss, totals[1])
```

```python
import functools
from types import SimpleNamespace

import jax
import jax.numpy as jnp
from jax import lax
from jax.experimental import pallas as pl
from jax.experimental.pallas import tpu as pltpu
from jax.sharding import PartitionSpec as P

HT = 4096
GROUP = 128
HEAD = 128
EPS = 1e-06
F32, BF16 = jnp.float32, jnp.bfloat16
MESH = pl.DeviceIdType.MESH

N = 8
ZH = 4
LEAD = 64
QW = 1792
KVW = 256
WIDE = QW + 128
HALF = QW // 2
TAIL = 16


def scratch_spec():
    dma, vmem = pltpu.SemaphoreType.DMA, pltpu.VMEM
    return dict(
        codes_sib=vmem((512, 1024), jnp.int32),
        perm=vmem((8, 1024, 128), jnp.int32),
        xb=vmem((2, 4, 32, 512), BF16),
        resb=vmem((2, 4, 32, 512), BF16),
        gainb=vmem((2, 8, 512), F32),
        scraw=vmem((2, 64, 512), F32),
        scp=vmem((2, 64, 512), F32),
        spread=vmem((512, 512), BF16),
        wbuf=vmem((1024, 1024), BF16),
        part=vmem((ZH, 128, 1024), BF16),
        relay=vmem((2, 64, 1024), BF16),
        near=vmem((2, 64, 1024), BF16),
        added=vmem((2, 64, 1024), BF16),
        summed=vmem((2, 64, 1024), BF16),
        proj=vmem((2, 8, 64, QW), BF16),
        pbuf=vmem((ZH, 32, WIDE), BF16),
        relay4=vmem((2, 16, WIDE), BF16),
        near4=vmem((2, 16, WIDE), BF16),
        added4=vmem((2, 16, WIDE), BF16),
        summed4=vmem((2, 16, WIDE), BF16),
        osend=vmem((8, 16, HALF), BF16),
        trecv=vmem((8, 16, HALF), BF16),
        q=vmem((LEAD, QW), BF16),
        k=vmem((LEAD, KVW), BF16),
        sb=vmem((8, LEAD, KVW), BF16),
        vw=vmem((8, 32, KVW), BF16),
        pvs=vmem((8, LEAD, KVW), BF16),
        pvr=vmem((8, LEAD, KVW), BF16),
        probs=vmem((2, 7 * LEAD, LEAD), BF16),
        att=vmem((2, 7 * LEAD, HEAD), F32),
        g1=vmem((8, LEAD + TAIL, KVW), BF16),
        g2s=vmem((8, 32 + TAIL, KVW), BF16),
        g2r=vmem((8, 32 + TAIL, KVW), BF16),
        g3=vmem((8, 32 + TAIL, KVW), BF16),
        qk_sem=dma((2,)),
        sib_s=dma((5,)),
        sib_r=dma((5,)),
        p_s=dma((10,)),
        p_r=dma((8, 2)),
        psib_r=dma((1,)),
        t1_s=dma((6,)),
        t1_r=dma((6,)),
        t4_s=dma((6,)),
        t4_r=dma((6,)),
        stu_s=dma((8,)),
        stu_r=dma((8,)),
        vw_s=dma((8,)),
        vw_r=dma((8,)),
        pv_s=dma((8,)),
        pv_r=dma((8,)),
        t5_s=dma((8,)),
        t5_r=dma((8,)),
        g1_s=dma((8,)),
        g1_r=dma((8,)),
        g2_s=dma((8,)),
        g2_r=dma((8,)),
        g3_s=dma((8,)),
        g3_r=dma((8,)),
    )


def dot(a, b, dims=((1,), (0,))):
    return lax.dot_general(a, b, (dims, ((), ())), preferred_element_type=F32)


def remote(src, dst, send, recv, **device):
    return pltpu.make_async_remote_copy(
        src_ref=src,
        dst_ref=dst,
        send_sem=send,
        recv_sem=recv,
        device_id=device,
        device_id_type=MESH,
    )


class Exchange:
    def __init__(self, axis, me, src, dst, send, recv):
        self.axis, self.me, self.src, self.dst = axis, me, src, dst
        self.send, self.recv = send, recv

    def each(self, act):
        def body(step, carry):
            act(lax.rem(self.me + step, N))
            return carry

        lax.fori_loop(1, N, body, 0)

    def copy(self, peer, slot):
        return remote(
            self.src(peer),
            self.dst.at[slot],
            self.send.at[peer],
            self.recv.at[slot],
            **{self.axis: peer},
        )

    def start(self):
        self.each(lambda peer: self.copy(peer, self.me).start())

    def wait_recv(self):
        self.each(lambda peer: self.copy(peer, peer).wait_recv())

    def wait_send(self):
        self.each(lambda peer: self.copy(peer, self.me).wait_send())


def split_sum(total):
    high = total.astype(BF16).astype(F32)
    lane = lax.broadcasted_iota(jnp.int32, (total.shape[0], 128), 1)
    return jnp.where(lane == 0, high, jnp.where(lane == 1, total - high, 0.0)).astype(BF16)


def split_scalar(value):
    row = lax.broadcasted_iota(jnp.int32, (TAIL, KVW), 0)
    lane = lax.broadcasted_iota(jnp.int32, (TAIL, KVW), 1)
    spread = jnp.full((TAIL, KVW), value, F32)
    high = spread.astype(BF16).astype(F32)
    rest = spread - high
    middle = rest.astype(BF16).astype(F32)
    low = rest - middle
    picked = jnp.where(lane == 0, high, jnp.where(lane == 1, middle, jnp.where(lane == 2, low, 0.0)))
    return jnp.where(row == 0, picked, 0.0).astype(BF16)


def add_wide(a, b):
    a, b = a.astype(F32), b.astype(F32)
    power = jnp.sum(a[:, QW:], axis=1, keepdims=True) + jnp.sum(b[:, QW:], axis=1, keepdims=True)
    return (a[:, :QW] + b[:, :QW]).astype(BF16), split_sum(power)


def kernel(
    total_count,
    names,
    x_ref,
    codes_ref,
    scales_ref,
    resid_ref,
    gain_ref,
    proj_ref,
    routes_ref,
    stu_ref,
    allow_ref,
    vw_ref,
    q_ref,
    k_ref,
    loss_ref,
    grad_ref,
    *scratch,
):
    m = SimpleNamespace(**dict(zip(names, scratch)))
    d, f, t = lax.axis_index("dp"), lax.axis_index("fsdp"), lax.axis_index("tensor")
    zh, c = lax.div(t, 2), lax.rem(t, 2)
    other = 1 - c
    sib = t + 1 - 2 * c
    zp, zm = lax.rem(t + 2, N), lax.rem(t + 6, N)
    fz = f + 1 - 2 * lax.rem(f, 2)
    xp, xm = lax.rem(f + 2, N), lax.rem(f + 6, N)
    xpz, xmz = xp + 1 - 2 * lax.rem(xp, 2), xm + 1 - 2 * lax.rem(xm, 2)
    xf = lax.rem(f + 4, N)
    xfz = xf + 1 - 2 * lax.rem(xf, 2)

    barrier = pltpu.get_barrier_semaphore()

    def greet(step, carry):
        for axis, me in (("tensor", t), ("fsdp", f), ("dp", d)):
            pl.semaphore_signal(
                barrier, inc=1, device_id={axis: lax.rem(me + step, N)}, device_id_type=MESH
            )
        return carry

    lax.fori_loop(1, N, greet, 0)
    pl.semaphore_wait(barrier, 3 * (N - 1))

    sib_copies = [
        remote(codes_ref, m.codes_sib, m.sib_s.at[0], m.sib_r.at[0], tensor=sib),
        remote(x_ref.at[:, other], m.xb.at[c], m.sib_s.at[1], m.sib_r.at[1], tensor=sib),
        remote(scales_ref, m.scraw.at[c], m.sib_s.at[2], m.sib_r.at[2], tensor=sib),
        remote(resid_ref.at[:, other], m.resb.at[c], m.sib_s.at[3], m.sib_r.at[3], tensor=sib),
        remote(gain_ref, m.gainb.at[c], m.sib_s.at[4], m.sib_r.at[4], tensor=sib),
    ]
    sib_waits = [
        remote(codes_ref, m.codes_sib, m.sib_s.at[0], m.sib_r.at[0], tensor=sib),
        remote(x_ref.at[:, other], m.xb.at[other], m.sib_s.at[1], m.sib_r.at[1], tensor=sib),
        remote(scales_ref, m.scraw.at[other], m.sib_s.at[2], m.sib_r.at[2], tensor=sib),
        remote(resid_ref.at[:, other], m.resb.at[other], m.sib_s.at[3], m.sib_r.at[3], tensor=sib),
        remote(gain_ref, m.gainb.at[other], m.sib_s.at[4], m.sib_r.at[4], tensor=sib),
    ]
    for copy in sib_copies:
        copy.start()

    def block(owner):
        return m.proj.at[c, owner]

    def half_block(owner, half):
        return m.proj.at[c, owner, pl.ds(32 * half, 32)]

    to_z = remote(proj_ref, block(f), m.p_s.at[0], m.p_r.at[f, 0], fsdp=fz)
    to_x = [
        remote(proj_ref, block(f), m.p_s.at[1], m.p_r.at[f, 0], fsdp=xp),
        remote(proj_ref, block(f), m.p_s.at[2], m.p_r.at[f, 0], fsdp=xm),
    ]
    to_xz = [
        remote(block(fz), block(fz), m.p_s.at[3], m.p_r.at[fz, 0], fsdp=xp),
        remote(block(fz), block(fz), m.p_s.at[4], m.p_r.at[fz, 0], fsdp=xm),
    ]
    forward = [
        remote(half_block(xm, 0), half_block(xm, 0), m.p_s.at[5], m.p_r.at[xm, 0], fsdp=xp),
        remote(half_block(xp, 1), half_block(xp, 1), m.p_s.at[6], m.p_r.at[xp, 1], fsdp=xm),
        remote(half_block(xmz, 0), half_block(xmz, 0), m.p_s.at[7], m.p_r.at[xmz, 0], fsdp=xp),
        remote(half_block(xpz, 1), half_block(xpz, 1), m.p_s.at[8], m.p_r.at[xpz, 1], fsdp=xm),
    ]

    def arrived(owner):
        return remote(proj_ref, block(owner), m.p_s.at[0], m.p_r.at[owner, 0], fsdp=fz)

    def arrived_half(owner, half):
        return remote(
            half_block(owner, half), half_block(owner, half), m.p_s.at[5], m.p_r.at[owner, half], fsdp=xp
        )

    to_sib = remote(m.proj.at[c], m.proj.at[c], m.p_s.at[9], m.psib_r.at[0], tensor=sib)
    from_sib = remote(m.proj.at[other], m.proj.at[other], m.p_s.at[9], m.psib_r.at[0], tensor=sib)
    to_z.start()
    for copy in to_x:
        copy.start()

    students = Exchange("fsdp", f, lambda peer: stu_ref.at[peer], m.sb, m.stu_s, m.stu_r)
    value_rows = Exchange("tensor", t, lambda peer: vw_ref, m.vw, m.vw_s, m.vw_r)
    value_parts = Exchange("fsdp", f, lambda peer: m.pvs.at[peer], m.pvr, m.pv_s, m.pv_r)
    targets = Exchange("dp", d, lambda peer: m.osend.at[peer], m.trecv, m.t5_s, m.t5_r)
    grads1 = Exchange("fsdp", f, lambda peer: m.g1.at[f], m.g1, m.g1_s, m.g1_r)
    grads2 = Exchange("tensor", t, lambda peer: m.g2s.at[peer], m.g2r, m.g2_s, m.g2_r)
    grads3 = Exchange("dp", d, lambda peer: m.g3.at[d], m.g3, m.g3_s, m.g3_r)
    students.start()
    value_rows.start()
    queries_in = pltpu.make_async_copy(q_ref.at[pl.ds(0, LEAD)], m.q, m.qk_sem.at[0])
    keys_in = pltpu.make_async_copy(k_ref.at[pl.ds(0, LEAD)], m.k, m.qk_sem.at[1])
    queries_in.start()
    keys_in.start()

    for b in range(4):
        m.xb[c, b] = x_ref[b, c]
        m.resb[c, b] = resid_ref[b, c]
    m.gainb[c] = gain_ref[...]
    m.scraw[c] = scales_ref[...]
    m.proj[c, f] = proj_ref[...]
    m.sb[f] = stu_ref[f]
    m.vw[t] = vw_ref[...]

    row = lax.broadcasted_iota(jnp.int32, (512, 512), 0)
    col = lax.broadcasted_iota(jnp.int32, (512, 512), 1)
    own_order = ((row >> 4) & 7) * 64 + (row & 15) * 4 + (row >> 7)
    m.spread[...] = jnp.where(own_order == col, 1.0, 0.0).astype(BF16)

    def shuffle(src, slot):
        lane = lax.broadcasted_iota(jnp.int32, (32, 128), 1)

        def body(i, carry):
            at = pl.multiple_of(i * 32, 32)
            a = [src[pl.ds(at, 32), j * 128 : (j + 1) * 128] for j in range(8)]
            for step in (4, 2, 1):
                upper = (lane & (16 * step)) != 0
                new = list(a)
                for j in range(8):
                    if j & step == 0:
                        low, high = a[j], a[j + step]
                        new[j] = jnp.where(upper, pltpu.roll(high, 16 * step, 1), low)
                        new[j + step] = jnp.where(upper, high, pltpu.roll(low, 128 - 16 * step, 1))
                a = new
            for j in range(8):
                m.perm[j, pl.ds(pl.multiple_of(slot * 512 + i * 32, 32), 32), :] = a[j]
            return carry

        lax.fori_loop(0, 16, body, 0)

    shuffle(codes_ref, c)
    for copy in sib_waits:
        copy.wait_recv()
    shuffle(m.codes_sib, other)
    for slot in range(2):
        m.scp[slot] = dot(m.scraw[slot].astype(BF16), m.spread[...], ((1,), (1,)))

    def partial(r):
        z = lax.rem(zh + r, ZH)

        def body(i, carry):
            s, src = lax.div(i, 2), lax.rem(i, 2)
            slice_at = 2 * z + s
            sc = m.scp[src, pl.ds(pl.multiple_of(slice_at * 8, 8), 8), :]
            for g in range(4):
                at = pl.multiple_of(src * 512 + g * GROUP, GROUP)
                words = m.perm[slice_at, pl.ds(at, GROUP), :]
                for level in range(4):
                    value = (lax.shift_right_logical(words, 4 * level) & 15).astype(F32) - 8.0
                    value = value * sc[g : g + 1, level * 128 : (level + 1) * 128]
                    lanes = pl.ds(pl.multiple_of(s * 512 + level * 128, 128), 128)
                    m.wbuf[pl.ds(at, GROUP), lanes] = value.astype(BF16)
            return carry

        lax.fori_loop(0, 4, body, 0)
        x0 = m.xb[0].reshape(128, 512)
        x1 = m.xb[1].reshape(128, 512)
        for s in range(2):
            lanes = slice(s * 512, (s + 1) * 512)
            acc = dot(x0, m.wbuf[0:512, lanes]) + dot(x1, m.wbuf[512:1024, lanes])
            m.part[r, :, lanes] = dot(acc.astype(BF16), m.spread[...]).astype(BF16)

    def ring(src, relay, near, added, summed, send, recv, half):
        low, high = pl.ds(0, half), pl.ds(half, half)
        far = [
            remote(src(2, low), relay.at[0], send.at[0], recv.at[0], tensor=zp),
            remote(src(2, high), relay.at[1], send.at[1], recv.at[1], tensor=zm),
        ]
        direct = [
            remote(src(1, high), near.at[0], send.at[2], recv.at[2], tensor=zp),
            remote(src(3, low), near.at[1], send.at[3], recv.at[3], tensor=zm),
        ]
        sums = [
            remote(added.at[0], summed.at[0], send.at[4], recv.at[4], tensor=zp),
            remote(added.at[1], summed.at[1], send.at[5], recv.at[5], tensor=zm),
        ]
        return far, direct, sums

    far, direct, sums = ring(
        lambda r, rows: m.part.at[r, rows], m.relay, m.near, m.added, m.summed, m.t1_s, m.t1_r, 64
    )
    partial(2)
    far[0].start()
    far[1].start()
    arrived(fz).wait_recv()
    for copy in to_xz:
        copy.start()
    partial(1)
    direct[0].start()
    partial(3)
    direct[1].start()

    students.wait_recv()
    value_rows.wait_recv()
    rows_of_value = m.vw[...].reshape(8 * 32, KVW)
    value_part = dot(m.sb[...].reshape(8 * LEAD, KVW), rows_of_value)
    m.pvs[...] = value_part.reshape(8, LEAD, KVW).astype(BF16)
    m.pvr[f] = m.pvs[f]
    value_parts.start()
    far[0].wait_recv()
    m.added[0] = (m.part[1, 0:64].astype(F32) + m.relay[0].astype(F32)).astype(BF16)
    sums[0].start()
    far[1].wait_recv()
    m.added[1] = (m.part[3, 64:128].astype(F32) + m.relay[1].astype(F32)).astype(BF16)
    sums[1].start()
    partial(0)

    for owner in (xm, xp, xmz, xpz):
        arrived(owner).wait_recv()
    for copy in forward:
        copy.start()

    queries_in.wait()
    keys_in.wait()
    allow = jnp.concatenate([allow_ref[...]] * 7, axis=0)
    for g in range(2):
        heads = [m.q[:, (g * 7 + h) * HEAD : (g * 7 + h + 1) * HEAD] for h in range(7)]
        scores = dot(jnp.concatenate(heads, axis=0), m.k[:, g * HEAD : (g + 1) * HEAD], ((1,), (1,)))
        scores = jnp.where(allow > 0.0, scores * HEAD ** (-0.5), -1e30)
        weights = jnp.exp(scores - jnp.max(scores, axis=1, keepdims=True))
        m.probs[g] = (weights / jnp.sum(weights, axis=1, keepdims=True)).astype(BF16)
    value_parts.wait_recv()
    values = m.pvr[0].astype(F32)
    for j in range(1, 8):
        values = values + m.pvr[j].astype(F32)
    values = values.astype(BF16)
    for g in range(2):
        m.att[g] = dot(m.probs[g], values[:, g * HEAD : (g + 1) * HEAD])

    for owner in (xf, xfz):
        for half in range(2):
            arrived_half(owner, half).wait_recv()
    to_sib.start()

    for copy in direct:
        copy.wait_recv()
    for copy in sums:
        copy.wait_recv()
    from_sib.wait_recv()
    lower = m.part[0, 0:64].astype(F32) + m.summed[0].astype(F32) + m.near[1].astype(F32)
    upper = m.part[0, 64:128].astype(F32) + m.near[0].astype(F32) + m.summed[1].astype(F32)
    out = jnp.concatenate([lower, upper], axis=0)
    power = jnp.zeros((128, 1), F32)
    scaled = []
    for s in range(2):
        hidden = out[:, s * 512 : (s + 1) * 512] + m.resb[s].reshape(128, 512).astype(F32)
        power = power + jnp.sum(hidden * hidden, axis=1, keepdims=True)
        scaled.append((hidden * m.gainb[s, 0:1, :]).astype(BF16))
    m.pbuf[:, :, QW:] = split_sum(power).reshape(ZH, 32, 128)
    for j in range(7):
        lanes = slice(j * 256, (j + 1) * 256)
        acc = dot(scaled[0], m.proj[0, :, :, lanes].reshape(512, 256))
        acc = acc + dot(scaled[1], m.proj[1, :, :, lanes].reshape(512, 256))
        m.pbuf[:, :, lanes] = acc.astype(BF16).reshape(ZH, 32, 256)

    far4, direct4, sums4 = ring(
        lambda r, rows: m.pbuf.at[lax.rem(zh + r, ZH), rows],
        m.relay4,
        m.near4,
        m.added4,
        m.summed4,
        m.t4_s,
        m.t4_r,
        16,
    )
    for copy in far4 + direct4:
        copy.start()

    row = lax.broadcasted_iota(jnp.int32, (64, 32), 0)
    col = lax.broadcasted_iota(jnp.int32, (64, 32), 1)
    place = ((d * N + f) * N + t) * 4
    wanted = jnp.full((64, 32), -1, jnp.int32)
    for j in range(4):
        wanted = jnp.where((col >> 3) == j, routes_ref[place + j], wanted)
    select = jnp.where(((row >> 3) == wanted) & ((row & 7) == (col & 7)), 1.0, 0.0).astype(BF16)
    lead = lax.broadcasted_iota(jnp.int32, (LEAD, HEAD), 0) >> 3
    mask = jnp.zeros((LEAD, HEAD), F32)
    for source in range(N):
        for j in range(4):
            hit = routes_ref[((source * N + f) * N + t) * 4 + j] == d
            mask = jnp.where(lead == source, jnp.maximum(mask, jnp.where(hit, 1.0, 0.0)), mask)

    far4[0].wait_recv()
    m.added4[0, :, :QW], m.added4[0, :, QW:] = add_wide(m.pbuf[lax.rem(zh + 1, ZH), 0:16], m.relay4[0])
    sums4[0].start()
    far4[1].wait_recv()
    m.added4[1, :, :QW], m.added4[1, :, QW:] = add_wide(m.pbuf[lax.rem(zh + 3, ZH), 16:32], m.relay4[1])
    sums4[1].start()
    for copy in direct4 + sums4:
        copy.wait_recv()
    own = m.pbuf[zh].astype(F32)
    lower = own[0:16] + m.summed4[0].astype(F32) + m.near4[1].astype(F32)
    upper = own[16:32] + m.near4[0].astype(F32) + m.summed4[1].astype(F32)
    total = jnp.concatenate([lower, upper], axis=0)
    power = jnp.sum(total[:, QW:], axis=1, keepdims=True)
    target = (total[:, :QW] * lax.rsqrt(power / HT + EPS)).astype(BF16)
    routed = dot(select, target)
    m.osend[...] = jnp.concatenate(
        [routed[:, :HALF].reshape(8, 8, HALF), routed[:, HALF:].reshape(8, 8, HALF)], axis=1
    ).astype(BF16)
    m.trecv[d] = m.osend[d]
    targets.start()
    targets.wait_recv()

    received = m.trecv[...].astype(F32)
    halves = [received[:, 0:8].reshape(LEAD, HALF), received[:, 8:16].reshape(LEAD, HALF)]
    lost = jnp.zeros((LEAD, HEAD), F32)
    for g in range(2):
        pieces = []
        for h in range(7):
            wanted = halves[g][:, h * HEAD : (h + 1) * HEAD]
            diff = m.att[g, h * LEAD : (h + 1) * LEAD] - wanted
            masked = diff * mask
            lost = lost + masked * diff
            pieces.append((2.0 * masked / QW).astype(BF16))
        grad = dot(m.probs[g], jnp.concatenate(pieces, axis=0), ((0,), (0,)))
        m.g1[f, 0:LEAD, g * HEAD : (g + 1) * HEAD] = grad.astype(BF16)
    m.g1[f, LEAD:] = split_scalar(jnp.sum(lost))
    grads1.start()
    grads1.wait_recv()
    grad = dot(
        m.sb[...].reshape(8 * LEAD, KVW), m.g1[:, 0:LEAD, :].reshape(8 * LEAD, KVW), ((0,), (0,))
    )
    m.g2s[:, 0:32, :] = grad.reshape(8, 32, KVW).astype(BF16)
    loss_tail = split_scalar(jnp.sum(m.g1[:, LEAD:, :].astype(F32)))
    for j in range(N):
        m.g2s[j, 32:, :] = loss_tail
    m.g2r[t] = m.g2s[t]
    grads2.start()
    grads2.wait_recv()
    m.g3[d, 0:32, :] = jnp.sum(m.g2r[:, 0:32, :].astype(F32), axis=0).astype(BF16)
    m.g3[d, 32:, :] = split_scalar(jnp.sum(m.g2r[:, 32:, :].astype(F32)))
    grads3.start()
    grads3.wait_recv()
    grad_ref[...] = jnp.sum(m.g3[:, 0:32, :].astype(F32), axis=0)
    loss_ref[0, 0] = jnp.sum(m.g3[:, 32:, :].astype(F32)) / total_count

    for copy in sib_copies + [to_z] + to_x + to_xz + forward + [to_sib]:
        copy.wait_send()
    for copy in far + direct + sums + far4 + direct4 + sums4:
        copy.wait_send()
    for exchange in (students, value_rows, value_parts, targets, grads1, grads2, grads3):
        exchange.wait_send()


def local(
    teacher_in,
    codes,
    scales,
    teacher_resid,
    teacher_gain,
    projector,
    routes,
    student_in,
    queries,
    keys,
    segments,
    value_weight,
):
    x = teacher_in.reshape(4, 2, 32, 512)
    resid = teacher_resid.reshape(4, 2, 32, 512)
    gain = jnp.broadcast_to(teacher_gain.astype(F32).reshape(1, 512), (8, 512))
    by_slice = scales.astype(F32).reshape(4, 8, 8, 64).transpose(2, 0, 1, 3).reshape(8, 4, 512)
    by_slice = jnp.pad(by_slice, ((0, 0), (0, 4), (0, 0))).reshape(64, 512)
    lead = student_in[:LEAD].reshape(LEAD, 8, 8, 28)
    lead = jnp.pad(lead, ((0, 0), (0, 0), (0, 0), (0, 4))).transpose(1, 0, 2, 3).reshape(8, LEAD, 256)
    rows = segments[:LEAD]
    places = jnp.arange(LEAD, dtype=jnp.int32)
    allow = (rows[:, None] == rows[None, :]) & (places[:, None] >= places[None, :])
    value_rows = jnp.pad(value_weight, ((0, 4), (0, 0)))
    spec = scratch_spec()
    vmem = pl.BlockSpec(memory_space=pltpu.VMEM)
    smem = pl.BlockSpec(memory_space=pltpu.SMEM)
    anywhere = pl.BlockSpec(memory_space=pl.ANY)
    loss, grad = pl.pallas_call(
        functools.partial(kernel, float(16384 * QW), tuple(spec)),
        out_shape=(
            jax.ShapeDtypeStruct((1, 1), F32),
            jax.ShapeDtypeStruct((32, KVW), F32),
        ),
        in_specs=[vmem] * 6 + [smem] + [vmem] * 3 + [anywhere] * 2,
        out_specs=(smem, vmem),
        scratch_shapes=list(spec.values()),
        compiler_params=pltpu.CompilerParams(
            collective_id=0, has_side_effects=True, vmem_limit_bytes=48 * 1024 * 1024
        ),
        name="distill",
    )(
        x,
        codes,
        by_slice,
        resid,
        gain,
        projector.reshape(64, QW),
        routes.reshape(2048),
        lead,
        allow.astype(F32),
        value_rows,
        queries,
        keys,
    )
    return loss[0, 0], grad[:28]


def solution(mesh):
    return jax.shard_map(
        local,
        mesh=mesh,
        in_specs=(
            P(("dp", "fsdp"), "tensor"),
            P("tensor", None),
            P("tensor", None),
            P(("dp", "fsdp"), None, "tensor"),
            P(None, "tensor"),
            P("fsdp", "tensor", None),
            P(),
            P(("dp", "fsdp", "tensor"), None),
            P(("dp", "fsdp", "tensor"), None),
            P(("dp", "fsdp", "tensor"), None),
            P(("dp", "fsdp", "tensor")),
            P(("fsdp", "tensor"), None),
        ),
        out_specs=(P(), P(("fsdp", "tensor"), None)),
        check_vma=False,
    )
```

```python
import functools
from types import SimpleNamespace

import jax
import jax.numpy as jnp
from jax import lax
from jax.experimental import pallas as pl
from jax.experimental.pallas import tpu as pltpu
from jax.sharding import PartitionSpec as P

HT = 4096
GROUP = 128
HEAD = 128
EPS = 1e-06
F32, BF16 = jnp.float32, jnp.bfloat16
MESH = pl.DeviceIdType.MESH

N = 8
ZH = 4
LEAD = 64
QW = 1792
KVW = 256
CHUNKS = (1024, 768)
WIDTHS = (1024 + 128, 768)
LOSS_ROW = 28


def ring_buffers(name, rows, width):
    block, sems = pltpu.VMEM((2, rows, width), BF16), pltpu.SemaphoreType.DMA((6,))
    spec = {f"{name}_{part}": block for part in ("relay", "near", "added", "summed")}
    return spec | {f"{name}_s": sems, f"{name}_r": sems}


def scratch_spec():
    dma, vmem = pltpu.SemaphoreType.DMA, pltpu.VMEM
    return dict(
        codes=vmem((512, 1024), jnp.int32),
        routes=pltpu.SMEM((2048,), jnp.int32),
        x=vmem((4, 2, 32, 512), BF16),
        xb=vmem((2, 4, 32, 512), BF16),
        stu=vmem((LEAD, QW), BF16),
        stus=vmem((8, LEAD, KVW), BF16),
        residt=vmem((512, 256), BF16),
        resid=vmem((4, 2, 32, 512), BF16),
        resb=vmem((2, 4, 32, 512), BF16),
        gainb=vmem((2, 8, 512), F32),
        vwp=vmem((32, KVW), BF16),
        vw=vmem((8, 32, KVW), BF16),
        perm=vmem((8, 256, 128), jnp.int32),
        scp=vmem((64, 512), F32),
        spread=vmem((512, 512), BF16),
        wbuf=vmem((512, 1024), BF16),
        part=vmem((ZH, 128, 1024), BF16),
        half_out=vmem((ZH, 128, 1024), BF16),
        half_in=vmem((ZH, 128, 1024), BF16),
        proj=vmem((2, 2, 4, 64, QW), BF16),
        q=vmem((LEAD, QW), BF16),
        k=vmem((LEAD, KVW), BF16),
        sb=vmem((8, LEAD, KVW), BF16),
        pvs=vmem((8, LEAD, KVW), BF16),
        pvr=vmem((8, LEAD, KVW), BF16),
        probs=vmem((2, 7 * LEAD, LEAD), BF16),
        g1=vmem((8, LEAD, KVW), BF16),
        lost=vmem((8, 8, 128), F32),
        g2s=vmem((8, 32, KVW), BF16),
        g2r=vmem((8, 32, KVW), BF16),
        g3=vmem((8, 32, KVW), BF16),
        **ring_buffers("t1", 64, 1024),
        **{f"pbuf{i}": vmem((ZH, 32, width), BF16) for i, width in enumerate(WIDTHS)},
        **ring_buffers("t4a", 16, WIDTHS[0]),
        **ring_buffers("t4b", 16, WIDTHS[1]),
        **{f"osend{i}": vmem((8, 16, width // 2), BF16) for i, width in enumerate(CHUNKS)},
        **{f"trecv{i}": vmem((8, 16, width // 2), BF16) for i, width in enumerate(CHUNKS)},
        in_sem=dma((8,)),
        sib_s=dma((6,)),
        sib_r=dma((6,)),
        p_s=dma((9,)),
        p_r=dma((8, 2)),
        psib_s=dma((8,)),
        psib_r=dma((8,)),
        **{
            name + end: dma((8,))
            for name in ("py", "stu", "vwz", "vwy", "pv", "t5a", "t5b", "g1", "loss", "g2", "g3")
            for end in ("_s", "_r")
        },
    )


def dot(a, b, dims=((1,), (0,))):
    return lax.dot_general(a, b, (dims, ((), ())), preferred_element_type=F32)


def remote(src, dst, send, recv, **device):
    return pltpu.make_async_remote_copy(
        src_ref=src,
        dst_ref=dst,
        send_sem=send,
        recv_sem=recv,
        device_id=device,
        device_id_type=MESH,
    )


class Flow:
    def __init__(self):
        self.sent, self.due = [], []

    def start(self, *copies, due=()):
        for copy in copies:
            copy.start()
        self.sent += copies
        self.due += list(due)

    def wait(self, *copies):
        for copy in copies:
            copy.wait_recv()
            self.due = [left for left in self.due if left is not copy]

    def finish(self):
        for copy in list(self.due):
            self.wait(copy)
        for copy in self.sent:
            copy.wait_send()


class Exchange:
    def __init__(self, axis, me, src, dst, send, recv):
        self.axis, self.me, self.src, self.dst = axis, me, src, dst
        self.send, self.recv = send, recv

    def each(self, act):
        def body(step, carry):
            act(lax.rem(self.me + step, N))
            return carry

        lax.fori_loop(1, N, body, 0)

    def copy(self, peer, slot):
        return remote(
            self.src(peer),
            self.dst(slot),
            self.send.at[peer],
            self.recv.at[slot],
            **{self.axis: peer},
        )

    def start(self):
        self.each(lambda peer: self.copy(peer, self.me).start())

    def wait_recv(self):
        self.each(lambda peer: self.copy(peer, peer).wait_recv())

    def wait_send(self):
        self.each(lambda peer: self.copy(peer, self.me).wait_send())


def split_sum(total):
    high = total.astype(BF16).astype(F32)
    lane = lax.broadcasted_iota(jnp.int32, (total.shape[0], 128), 1)
    return jnp.where(lane == 0, high, jnp.where(lane == 1, total - high, 0.0)).astype(BF16)


def loss_row(value):
    row, lane = iotas(32, KVW)
    spread = jnp.full((32, KVW), value, F32)
    high = spread.astype(BF16).astype(F32)
    middle = (spread - high).astype(BF16).astype(F32)
    low = spread - high - middle
    picked = jnp.where(lane == 0, high, jnp.where(lane == 1, middle, jnp.where(lane == 2, low, 0.0)))
    return jnp.where(row == LOSS_ROW, picked, 0.0)


def loss_of(block):
    row, _ = iotas(32, KVW)
    return jnp.sum(jnp.where(row == LOSS_ROW, block, 0.0))


def ring_sum(out, at, mine, other, width):
    mine, other = mine.astype(F32), other.astype(F32)
    total = mine + other
    out[at, :, :width] = total[:, :width].astype(BF16)
    if out.shape[2] > width:
        out[at, :, width:] = split_sum(jnp.sum(total[:, width:], axis=1, keepdims=True))


def transpose_runs(a):
    lane = lax.broadcasted_iota(jnp.int32, a[0].shape, 1)
    for step in (4, 2, 1):
        upper = (lane & (16 * step)) != 0
        new = list(a)
        for j in range(8):
            if j & step == 0:
                low, high = a[j], a[j + step]
                new[j] = jnp.where(upper, pltpu.roll(high, 16 * step, 1), low)
                new[j + step] = jnp.where(upper, high, pltpu.roll(low, 128 - 16 * step, 1))
        a = new
    return a


def one_hot(hit):
    return jnp.where(hit, 1.0, 0.0).astype(BF16)


def iotas(*shape):
    return [lax.broadcasted_iota(jnp.int32, shape, axis) for axis in range(2)]


def kernel(
    total_count,
    names,
    x_ref,
    codes_ref,
    scales_ref,
    residt_ref,
    gain_ref,
    proj_ref,
    routes_ref,
    stu_ref,
    seg_ref,
    vw_ref,
    q_ref,
    k_ref,
    loss_ref,
    grad_ref,
    *scratch,
):
    m = SimpleNamespace(**dict(zip(names, scratch)))
    flow = Flow()

    d, f, t = lax.axis_index("dp"), lax.axis_index("fsdp"), lax.axis_index("tensor")
    zh, c = lax.div(t, 2), lax.rem(t, 2)
    other = 1 - c
    sib = t + 1 - 2 * c
    zp, zm = lax.rem(t + 2, N), lax.rem(t + 6, N)
    fz = f + 1 - 2 * lax.rem(f, 2)
    xp, xm = lax.rem(f + 2, N), lax.rem(f + 6, N)
    xpz, xmz = xp + 1 - 2 * lax.rem(xp, 2), xm + 1 - 2 * lax.rem(xm, 2)
    xf = lax.rem(f + 4, N)
    xfz = xf + 1 - 2 * lax.rem(xf, 2)

    barrier = pltpu.get_barrier_semaphore()

    def greet(step, carry):
        for axis, me in (("tensor", t), ("fsdp", f), ("dp", d)):
            pl.semaphore_signal(
                barrier, inc=1, device_id={axis: lax.rem(me + step, N)}, device_id_type=MESH
            )
        return carry

    lax.fori_loop(1, N, greet, 0)

    zl, xi = lax.rem(f, 2), lax.div(f, 2)
    inputs = [
        (codes_ref, m.codes),
        (x_ref, m.x),
        (stu_ref.at[pl.ds(0, LEAD)], m.stu),
        (proj_ref, m.proj.at[c, zl, xi]),
        (residt_ref, m.residt),
        (q_ref.at[pl.ds(0, LEAD)], m.q),
        (k_ref.at[pl.ds(0, LEAD)], m.k),
        (routes_ref, m.routes),
    ]
    inputs = [pltpu.make_async_copy(src, dst, m.in_sem.at[i]) for i, (src, dst) in enumerate(inputs)]
    codes_in, x_in, stu_in, proj_in, resid_in, q_in, k_in, routes_in = inputs
    for copy in inputs:
        copy.start()

    row, col = iotas(512, 512)
    own_order = ((row >> 4) & 7) * 64 + (row & 15) * 4 + (row >> 7)
    m.spread[...] = one_hot(own_order == col)

    scales = jnp.concatenate([scales_ref[...].astype(F32), jnp.zeros((4, HT), F32)], axis=0)
    scales = jnp.concatenate([scales[:, j * 512 : (j + 1) * 512] for j in range(8)], axis=0)
    scales = dot(scales.astype(BF16), m.spread[...], ((1,), (1,)))
    for level in range(4):
        lanes = slice(level * 128, (level + 1) * 128)
        for j, piece in enumerate(transpose_runs([scales[8 * j : 8 * j + 8, lanes] for j in range(8)])):
            m.scp[8 * j : 8 * j + 8, lanes] = piece

    def shuffle(i, carry):
        at = pl.ds(pl.multiple_of(i * 32, 32), 32)
        far_at = pl.ds(pl.multiple_of(i * 32 + 256, 32), 32)
        words = []
        for j in range(8):
            lanes = slice(j * 128, (j + 1) * 128)
            words.append(m.codes[at, lanes] | (m.codes[far_at, lanes] << 16))
        for j, piece in enumerate(transpose_runs(words)):
            m.perm[j, at, :] = piece
        return carry

    def slots(ref):
        return lambda slot: ref.at[slot]

    def block(owner):
        return m.proj.at[c, lax.rem(owner, 2), lax.div(owner, 2)]

    def half_block(owner, half):
        return m.proj.at[c, lax.rem(owner, 2), lax.div(owner, 2), pl.ds(32 * half, 32)]

    def piece_at(place):
        down, along = lax.div(place, 2), lax.rem(place, 2)
        return pl.ds(pl.multiple_of(down * 16, 16), 16), pl.ds(pl.multiple_of(along * 896, 128), 896)

    def piece(owner, place):
        return m.proj.at[(c, lax.rem(owner, 2), lax.div(owner, 2)) + piece_at(place)]

    def pass_on(i, owner, half=None, src=None, **device):
        dst = block(owner) if half is None else half_block(owner, half)
        return remote(dst if src is None else src, dst, m.p_s.at[i], m.p_r.at[owner, half or 0], **device)

    to_z = remote(proj_ref.at[piece_at(d)], piece(f, d), m.p_s.at[0], m.p_r.at[f, 0], fsdp=fz)
    from_z = remote(proj_ref.at[piece_at(d)], piece(fz, d), m.p_s.at[0], m.p_r.at[fz, 0], fsdp=fz)
    pieces = Exchange("dp", d, lambda peer: piece(fz, d), lambda slot: piece(fz, slot), m.py_s, m.py_r)
    near_same = [pass_on(1, owner, fsdp=fz) for owner in (xm, xp)]
    near_other = [pass_on(1, owner, fsdp=fz) for owner in (xmz, xpz)]
    far_same = [pass_on(1, xf, half, fsdp=fz) for half in range(2)]
    far_other = [pass_on(1, xfz, half, fsdp=fz) for half in range(2)]
    def block_to_sibling(owner, slot):
        dst = m.proj.at[slot, lax.rem(owner, 2), lax.div(owner, 2)]
        return remote(block(owner), dst, m.psib_s.at[owner], m.psib_r.at[owner], tensor=sib)

    owners = (f, xm, xp, xf, fz, xmz, xpz, xfz)
    proj_here = [block_to_sibling(owner, other) for owner in owners]

    def share(*places):
        flow.start(*(block_to_sibling(owners[i], c) for i in places), due=[proj_here[i] for i in places])

    value_rows = Exchange("tensor", t, lambda peer: m.vwp, slots(m.vw), m.vwz_s, m.vwz_r)
    value_slices = Exchange("dp", d, lambda peer: m.vw.at[d], slots(m.vw), m.vwy_s, m.vwy_r)

    class ValueRows:
        def start(self):
            @pl.when(t == d)
            def _():
                m.vw[d] = m.vwp[...]
                value_rows.start()

        def wait_recv(self):
            @pl.when(t != d)
            def _():
                value_rows.copy(d, d).wait_recv()

        def wait_send(self):
            @pl.when(t == d)
            def _():
                value_rows.wait_send()

    sent_rows = ValueRows()
    row, col = iotas(32, 28)
    m.vwp[...] = dot(one_hot(row == col), vw_ref[...]).astype(BF16)

    pl.semaphore_wait(barrier, 3 * (N - 1))
    flow.start(to_z, due=[from_z])
    flow.start(pass_on(1, f, src=proj_ref, fsdp=xp), pass_on(2, f, src=proj_ref, fsdp=xm), due=near_same)
    flow.start(sent_rows, due=[sent_rows])

    codes_in.wait()
    lax.fori_loop(0, 8, shuffle, 0, unroll=4)
    x_in.wait()
    for b in range(4):
        m.xb[0, b] = m.x[b, c]
        m.xb[1, b] = m.x[b, other]

    def partial(r):
        z = lax.rem(zh + r, ZH)

        def dequantize(s, carry):
            slice_at = 2 * z + s
            sc = m.scp[pl.ds(pl.multiple_of(slice_at * 8, 8), 8), :]
            for g in range(4):
                at = slice(g * GROUP, (g + 1) * GROUP)
                words = m.perm[slice_at, g % 2 * GROUP : (g % 2 + 1) * GROUP, :]
                for level in range(4):
                    value = lax.shift_right_logical(words, g // 2 * 16 + 4 * level) & 15
                    value = value.astype(F32) - 8.0
                    value = value * sc[g : g + 1, level * 128 : (level + 1) * 128]
                    lanes = pl.ds(pl.multiple_of(s * 512 + level * 128, 128), 128)
                    m.wbuf[at, lanes] = value.astype(BF16)
            return carry

        lax.fori_loop(0, 2, dequantize, 0)
        rows = m.xb[...].reshape(256, 512)
        for s in range(2):
            lanes = slice(s * 512, (s + 1) * 512)
            acc = dot(rows, m.wbuf[:, lanes]).astype(BF16)
            acc = dot(acc, m.spread[...]).astype(BF16)
            m.part[r, :, lanes] = acc[0:128]
            m.half_out[r, :, lanes] = acc[128:256]

    def to_sibling(i, src, dst):
        return remote(src, dst, m.sib_s.at[i], m.sib_r.at[i], tensor=sib)

    halves = [to_sibling(r, m.half_out.at[r], m.half_in.at[r]) for r in range(ZH)]
    resid_there = to_sibling(4, m.resid.at[:, other], m.resb.at[c])
    resid_here = to_sibling(4, m.resid.at[:, other], m.resb.at[other])
    gain_there = to_sibling(5, m.gainb.at[c], m.gainb.at[c])
    gain_here = to_sibling(5, m.gainb.at[c], m.gainb.at[other])

    def add_half(r):
        flow.wait(halves[r])
        m.part[r] = (m.part[r].astype(F32) + m.half_in[r].astype(F32)).astype(BF16)

    students = Exchange("fsdp", f, slots(m.stus), slots(m.sb), m.stu_s, m.stu_r)
    value_parts = Exchange("fsdp", f, slots(m.pvs), slots(m.pvr), m.pv_s, m.pv_r)
    targets = [
        Exchange("dp", d, slots(m.osend0), slots(m.trecv0), m.t5a_s, m.t5a_r),
        Exchange("dp", d, slots(m.osend1), slots(m.trecv1), m.t5b_s, m.t5b_r),
    ]
    grads1 = Exchange("fsdp", f, lambda peer: m.g1.at[f], slots(m.g1), m.g1_s, m.g1_r)
    losses = Exchange("fsdp", f, lambda peer: m.lost.at[f], slots(m.lost), m.loss_s, m.loss_r)
    grads2 = Exchange("tensor", t, slots(m.g2s), slots(m.g2r), m.g2_s, m.g2_r)
    grads3 = Exchange("dp", d, lambda peer: m.g3.at[d], slots(m.g3), m.g3_s, m.g3_r)

    def ring(src, name, half):
        relay, near, added, summed, send, recv = (
            getattr(m, f"{name}_{end}") for end in ("relay", "near", "added", "summed", "s", "r")
        )
        low, high = pl.ds(0, half), pl.ds(half, half)
        far = [
            remote(src(2, low), relay.at[0], send.at[0], recv.at[0], tensor=zp),
            remote(src(2, high), relay.at[1], send.at[1], recv.at[1], tensor=zm),
        ]
        direct = [
            remote(src(1, high), near.at[0], send.at[2], recv.at[2], tensor=zp),
            remote(src(3, low), near.at[1], send.at[3], recv.at[3], tensor=zm),
        ]
        sums = [
            remote(added.at[0], summed.at[0], send.at[4], recv.at[4], tensor=zp),
            remote(added.at[1], summed.at[1], send.at[5], recv.at[5], tensor=zm),
        ]
        return far, direct, sums

    far, direct, sums = ring(lambda r, rows: m.part.at[r, rows], "t1", 64)
    partial(2)
    flow.start(halves[2], due=[halves[2]])
    partial(1)
    flow.start(halves[1], due=[halves[1]])
    add_half(2)
    flow.start(*far, due=far)
    partial(3)
    flow.start(halves[3], due=[halves[3]])
    add_half(1)
    flow.start(direct[0], due=direct[:1])
    proj_in.wait()
    share(0)
    flow.wait(from_z, sent_rows)
    flow.start(pieces, due=[pieces])
    partial(0)
    flow.start(halves[0], due=[halves[0]])
    add_half(3)
    flow.start(direct[1], due=direct[1:])
    flow.start(value_slices, due=[value_slices])

    resid_in.wait()
    row, col = iotas(512, 512)
    m.resid[...] = dot(m.residt[...], one_hot(row == col), ((0,), (0,))).astype(BF16).reshape(4, 2, 32, 512)
    for b in range(4):
        m.resb[c, b] = m.resid[b, c]
    row, col = iotas(64, 512)
    gain = dot(gain_ref[...], one_hot((col & 63) == row))
    row, col = iotas(8, 512)
    gain = jnp.sum(jnp.where((col >> 6) == row, gain, 0.0), axis=0, keepdims=True)
    m.gainb[c] = jnp.broadcast_to(gain, (8, 512))
    flow.start(resid_there, gain_there, due=[resid_here, gain_here])
    add_half(0)

    flow.wait(*near_same)
    flow.start(pass_on(3, xm, 0, fsdp=xp), pass_on(4, xp, 1, fsdp=xm), due=far_same)
    share(1, 2)
    flow.wait(pieces)
    flow.start(pass_on(5, fz, fsdp=xp), pass_on(6, fz, fsdp=xm), due=near_other)
    share(4)
    flow.wait(far[0])
    ring_sum(m.t1_added, 0, m.part[1, 0:64], m.t1_relay[0], 1024)
    flow.start(sums[0], due=sums[:1])
    flow.wait(far[1])
    ring_sum(m.t1_added, 1, m.part[3, 64:128], m.t1_relay[1], 1024)
    flow.start(sums[1], due=sums[1:])

    stu_in.wait()
    row, col = iotas(896, 1024)
    pad = one_hot(((col >> 5) * 28 + (col & 31) == row) & ((col & 31) < 28))
    for j in range(2):
        padded = dot(m.stu[:, j * 896 : (j + 1) * 896], pad).astype(BF16)
        for i in range(4):
            m.stus[4 * j + i] = padded[:, i * KVW : (i + 1) * KVW]
    m.sb[f] = m.stus[f]

    places = jnp.broadcast_to(seg_ref[0:1, 0:128].astype(F32), (128, 128))
    same = places == jnp.transpose(places)
    row, col = iotas(128, 128)
    allow = jnp.where(same & (row >= col), 1.0, 0.0)[:LEAD, :LEAD]
    allow = jnp.concatenate([allow] * 7, axis=0)
    q_in.wait()
    k_in.wait()
    for g in range(2):
        heads = [m.q[:, (g * 7 + h) * HEAD : (g * 7 + h + 1) * HEAD] for h in range(7)]
        scores = dot(jnp.concatenate(heads, axis=0), m.k[:, g * HEAD : (g + 1) * HEAD], ((1,), (1,)))
        scores = jnp.where(allow > 0.0, scores * HEAD ** (-0.5), -1e30)
        weights = jnp.exp(scores - jnp.max(scores, axis=1, keepdims=True))
        m.probs[g] = (weights / jnp.sum(weights, axis=1, keepdims=True)).astype(BF16)

    routes_in.wait()
    row, col = iotas(64, 32)
    place = ((d * N + f) * N + t) * 4
    wanted = jnp.full((64, 32), -1, jnp.int32)
    for j in range(4):
        wanted = jnp.where((col >> 3) == j, m.routes[place + j], wanted)
    select = one_hot(((row >> 3) == wanted) & ((row & 7) == (col & 7)))
    lead = lax.broadcasted_iota(jnp.int32, (LEAD, HEAD), 0) >> 3
    mask = jnp.zeros((LEAD, HEAD), F32)
    for source in range(N):
        for j in range(4):
            hit = m.routes[((source * N + f) * N + t) * 4 + j] == d
            mask = jnp.where(lead == source, jnp.maximum(mask, jnp.where(hit, 1.0, 0.0)), mask)

    flow.wait(*far_same)
    share(3)
    flow.wait(*near_other)
    flow.start(pass_on(7, xmz, 0, fsdp=xp), pass_on(8, xpz, 1, fsdp=xm), due=far_other)
    share(5, 6)
    flow.wait(*direct, *sums, resid_here, gain_here)
    flow.start(students, due=[students])

    lower = m.part[0, 0:64].astype(F32) + m.t1_summed[0].astype(F32) + m.t1_near[1].astype(F32)
    upper = m.part[0, 64:128].astype(F32) + m.t1_near[0].astype(F32) + m.t1_summed[1].astype(F32)
    out = jnp.concatenate([lower, upper], axis=0)
    power = jnp.zeros((128, 1), F32)
    scaled = []
    for s in range(2):
        hidden = out[:, s * 512 : (s + 1) * 512] + m.resb[s].reshape(128, 512).astype(F32)
        power = power + jnp.sum(hidden * hidden, axis=1, keepdims=True)
        scaled.append((hidden * m.gainb[s, 0:1, :]).astype(BF16))
    m.pbuf0[:, :, CHUNKS[0] :] = split_sum(power).reshape(ZH, 32, 128)
    flow.wait(*far_other)
    share(7)
    flow.wait(*proj_here)

    def ahead(pbuf):
        return lambda r, rows: pbuf.at[lax.rem(zh + r, ZH), rows]

    rings = [ring(ahead(m.pbuf0), "t4a", 16), ring(ahead(m.pbuf1), "t4b", 16)]
    pbufs = (m.pbuf0, m.pbuf1)
    for i in range(2):
        for j in range(CHUNKS[i] // 256):
            lanes = slice(j * 256, (j + 1) * 256)
            from_lanes = slice(i * CHUNKS[0] + j * 256, i * CHUNKS[0] + (j + 1) * 256)
            acc = jnp.zeros((128, 256), F32)
            for s in range(2):
                rows = [m.proj[s, owner % 2, owner // 2, :, from_lanes] for owner in range(8)]
                acc = acc + dot(scaled[s], jnp.concatenate(rows, axis=0))
            pbufs[i][:, :, lanes] = acc.astype(BF16).reshape(ZH, 32, 256)
        flow.start(*rings[i][0], *rings[i][1], due=rings[i][0] + rings[i][1])
    for i, name in enumerate(("t4a", "t4b")):
        far4, direct4, sums4 = rings[i]
        relay, added = getattr(m, f"{name}_relay"), getattr(m, f"{name}_added")
        for way, r in enumerate((1, 3)):
            flow.wait(far4[way])
            mine = pbufs[i][lax.rem(zh + r, ZH), 16 * way : 16 * way + 16]
            ring_sum(added, way, mine, relay[way], CHUNKS[i])
            flow.start(sums4[way], due=[sums4[way]])

    flow.wait(students, value_slices)
    rows_of_value = m.vw[...].reshape(8 * 32, KVW)
    value_part = dot(m.sb[...].reshape(8 * LEAD, KVW), rows_of_value)
    m.pvs[...] = value_part.reshape(8, LEAD, KVW).astype(BF16)
    m.pvr[f] = m.pvs[f]

    row_scale = None
    for i, name in enumerate(("t4a", "t4b")):
        _, direct4, sums4 = rings[i]
        flow.wait(*direct4, *sums4)
        near, summed = getattr(m, f"{name}_near"), getattr(m, f"{name}_summed")
        own = pbufs[i][zh].astype(F32)
        lower = own[0:16] + summed[0].astype(F32) + near[1].astype(F32)
        upper = own[16:32] + near[0].astype(F32) + summed[1].astype(F32)
        total = jnp.concatenate([lower, upper], axis=0)
        if i == 0:
            power = jnp.sum(total[:, CHUNKS[0] :], axis=1, keepdims=True)
            row_scale = lax.rsqrt(power / HT + EPS)
        routed = dot(select, (total[:, : CHUNKS[i]] * row_scale).astype(BF16))
        half = CHUNKS[i] // 2
        osend, trecv = getattr(m, f"osend{i}"), getattr(m, f"trecv{i}")
        osend[...] = jnp.concatenate(
            [routed[:, :half].reshape(8, 8, half), routed[:, half:].reshape(8, 8, half)], axis=1
        ).astype(BF16)
        trecv[d] = osend[d]
        flow.start(targets[i], due=[targets[i]])
    flow.start(value_parts, due=[value_parts])
    flow.wait(value_parts)
    values = m.pvr[0].astype(F32)
    for j in range(1, 8):
        values = values + m.pvr[j].astype(F32)
    values = values.astype(BF16)
    attended = [dot(m.probs[g], values[:, g * HEAD : (g + 1) * HEAD]) for g in range(2)]

    lost = jnp.zeros((LEAD, HEAD), F32)
    pieces_of = ([], [])
    for i in range(2):
        flow.wait(targets[i])
        received = getattr(m, f"trecv{i}")[...].astype(F32)
        per_half = CHUNKS[i] // 2 // HEAD
        for j in range(2 * per_half):
            at, lane = j // per_half * 8, j % per_half * HEAD
            wanted = received[:, at : at + 8, lane : lane + HEAD].reshape(LEAD, HEAD)
            head = i * (CHUNKS[0] // HEAD) + j
            g, h = head // 7, head % 7
            diff = attended[g][h * LEAD : (h + 1) * LEAD] - wanted
            masked = diff * mask
            lost = lost + masked * diff
            pieces_of[g].append((2.0 * masked / QW).astype(BF16))
    for g in range(2):
        grad = dot(m.probs[g], jnp.concatenate(pieces_of[g], axis=0), ((0,), (0,)))
        m.g1[f, :, g * HEAD : (g + 1) * HEAD] = grad.astype(BF16)
    flow.start(grads1, due=[grads1])
    lost = lost.reshape(8, 8, 128).sum(axis=0)
    m.lost[f] = lost
    flow.start(losses, due=[losses])
    flow.wait(grads1)
    grad = dot(m.sb[...].reshape(8 * LEAD, KVW), m.g1[...].reshape(8 * LEAD, KVW), ((0,), (0,)))
    flow.wait(losses)
    tail = loss_row(jnp.sum(m.lost[...]))
    for j in range(N):
        m.g2s[j] = (grad[32 * j : 32 * j + 32] + tail).astype(BF16)
    m.g2r[t] = m.g2s[t]
    flow.start(grads2, due=[grads2])
    flow.wait(grads2)
    row, _ = iotas(32, KVW)
    total = jnp.sum(m.g2r[...].astype(F32), axis=0)
    m.g3[d] = jnp.where(row < LOSS_ROW, total, loss_row(loss_of(total))).astype(BF16)
    flow.start(grads3, due=[grads3])
    flow.wait(grads3)
    total = jnp.sum(m.g3[...].astype(F32), axis=0)
    grad_ref[...] = total[0:LOSS_ROW]
    loss_ref[0, 0] = loss_of(total) / total_count
    flow.finish()


def local(
    teacher_in,
    codes,
    scales,
    teacher_resid,
    teacher_gain,
    projector,
    routes,
    student_in,
    queries,
    keys,
    segments,
    value_weight,
):
    spec = scratch_spec()
    vmem = pl.BlockSpec(memory_space=pltpu.VMEM)
    smem = pl.BlockSpec(memory_space=pltpu.SMEM)
    hbm = pl.BlockSpec(memory_space=pltpu.HBM)
    loss, grad = pl.pallas_call(
        functools.partial(kernel, float(16384 * QW), tuple(spec)),
        out_shape=(
            jax.ShapeDtypeStruct((1, 1), F32),
            jax.ShapeDtypeStruct((28, KVW), F32),
        ),
        in_specs=[hbm, hbm, vmem, hbm, vmem, hbm, hbm, hbm, vmem, vmem, hbm, hbm],
        out_specs=(smem, vmem),
        scratch_shapes=list(spec.values()),
        compiler_params=pltpu.CompilerParams(
            collective_id=0, has_side_effects=True, vmem_limit_bytes=56 * 1024 * 1024
        ),
        name="distill",
    )(
        teacher_in.reshape(4, 2, 32, 512),
        codes,
        scales,
        teacher_resid.transpose(1, 2, 0).reshape(512, 256),
        teacher_gain,
        projector.reshape(64, QW),
        routes.reshape(2048),
        student_in,
        segments.reshape(1, 256),
        value_weight,
        queries,
        keys,
    )
    return loss[0, 0], grad


def solution(mesh):
    return jax.shard_map(
        local,
        mesh=mesh,
        in_specs=(
            P(("dp", "fsdp"), "tensor"),
            P("tensor", None),
            P("tensor", None),
            P(("dp", "fsdp"), None, "tensor"),
            P(None, "tensor"),
            P("fsdp", "tensor", None),
            P(),
            P(("dp", "fsdp", "tensor"), None),
            P(("dp", "fsdp", "tensor"), None),
            P(("dp", "fsdp", "tensor"), None),
            P(("dp", "fsdp", "tensor")),
            P(("fsdp", "tensor"), None),
        ),
        out_specs=(P(), P(("fsdp", "tensor"), None)),
        check_vma=False,
    )
```

```python
import functools
from types import SimpleNamespace

import jax
import jax.numpy as jnp
from jax import lax
from jax.experimental import pallas as pl
from jax.experimental.pallas import tpu as pltpu
from jax.sharding import PartitionSpec as P

HT = 4096
GROUP = 128
HEAD = 128
EPS = 1e-06
F32, BF16 = jnp.float32, jnp.bfloat16
MESH = pl.DeviceIdType.MESH

N = 8
ZH = 4
LEAD = 64
QW = 1792
KVW = 256
CHUNKS = (1024, 768)
WIDTHS = (1024 + 128, 768)
LOSS_ROW = 28


def ring_buffers(name, rows, width):
    block, sems = pltpu.VMEM((2, rows, width), BF16), pltpu.SemaphoreType.DMA((6,))
    spec = {f"{name}_{part}": block for part in ("relay", "near", "added", "summed")}
    return spec | {f"{name}_s": sems, f"{name}_r": sems}


def scratch_spec():
    dma, vmem = pltpu.SemaphoreType.DMA, pltpu.VMEM
    return dict(
        codes=vmem((512, 1024), jnp.int32),
        routes=pltpu.SMEM((2048,), jnp.int32),
        x=vmem((4, 2, 32, 512), BF16),
        xb=vmem((2, 4, 32, 512), BF16),
        stu=vmem((LEAD, QW), BF16),
        stus=vmem((8, LEAD, KVW), BF16),
        residt=vmem((512, 256), BF16),
        resid=vmem((4, 2, 32, 512), BF16),
        resb=vmem((2, 4, 32, 512), BF16),
        gainb=vmem((2, 8, 512), F32),
        vwp=vmem((32, KVW), BF16),
        vw=vmem((8, 32, KVW), BF16),
        perm=vmem((8, 256, 128), jnp.int32),
        scp=vmem((64, 512), F32),
        spread=vmem((512, 512), BF16),
        wbuf=vmem((512, 1024), BF16),
        part=vmem((ZH, 128, 1024), BF16),
        half_out=vmem((ZH, 128, 1024), BF16),
        half_in=vmem((ZH, 128, 1024), BF16),
        proj=vmem((2, 2, 4, 64, QW), BF16),
        q=vmem((LEAD, QW), BF16),
        k=vmem((LEAD, KVW), BF16),
        sb=vmem((8, LEAD, KVW), BF16),
        pvs=vmem((8, LEAD, KVW), BF16),
        pvr=vmem((8, LEAD, KVW), BF16),
        probs=vmem((2, 7 * LEAD, LEAD), BF16),
        probs_t=vmem((2, LEAD, 7 * LEAD), BF16),
        sb_t=vmem((KVW, 8 * LEAD), BF16),
        g1=vmem((8, LEAD, KVW), BF16),
        lost=vmem((8, 8, 128), F32),
        g2s=vmem((8, 32, KVW), BF16),
        g2r=vmem((8, 32, KVW), BF16),
        g3=vmem((8, 32, KVW), BF16),
        **ring_buffers("t1", 64, 1024),
        **{f"pbuf{i}": vmem((ZH, 32, width), BF16) for i, width in enumerate(WIDTHS)},
        **ring_buffers("t4a", 16, WIDTHS[0]),
        **ring_buffers("t4b", 16, WIDTHS[1]),
        **{f"osend{i}": vmem((8, 16, width // 2), BF16) for i, width in enumerate(CHUNKS)},
        **{f"trecv{i}": vmem((8, 16, width // 2), BF16) for i, width in enumerate(CHUNKS)},
        in_sem=dma((8,)),
        sib_s=dma((6,)),
        sib_r=dma((6,)),
        p_s=dma((9,)),
        p_r=dma((8, 2)),
        psib_s=dma((8,)),
        psib_r=dma((8,)),
        **{
            name + end: dma((8,))
            for name in ("stu", "vwz", "vwy", "pv", "t5a", "t5b", "g1", "loss", "g2", "g3")
            for end in ("_s", "_r")
        },
    )


def dot(a, b, dims=((1,), (0,))):
    return lax.dot_general(a, b, (dims, ((), ())), preferred_element_type=F32)


def remote(src, dst, send, recv, **device):
    return pltpu.make_async_remote_copy(
        src_ref=src,
        dst_ref=dst,
        send_sem=send,
        recv_sem=recv,
        device_id=device,
        device_id_type=MESH,
    )


class Flow:
    def __init__(self):
        self.sent, self.due = [], []

    def start(self, *copies, due=()):
        for copy in copies:
            copy.start()
        self.sent += copies
        self.due += list(due)

    def wait(self, *copies):
        for copy in copies:
            copy.wait_recv()
            self.due = [left for left in self.due if left is not copy]

    def finish(self):
        for copy in list(self.due):
            self.wait(copy)
        for copy in self.sent:
            copy.wait_send()


class Exchange:
    def __init__(self, axis, me, src, dst, send, recv):
        self.axis, self.me, self.src, self.dst = axis, me, src, dst
        self.send, self.recv = send, recv

    def each(self, act):
        def body(step, carry):
            act(lax.rem(self.me + step, N))
            return carry

        lax.fori_loop(1, N, body, 0)

    def copy(self, peer, slot):
        return remote(
            self.src(peer),
            self.dst(slot),
            self.send.at[peer],
            self.recv.at[slot],
            **{self.axis: peer},
        )

    def start(self):
        self.each(lambda peer: self.copy(peer, self.me).start())

    def wait_recv(self):
        self.each(lambda peer: self.copy(peer, peer).wait_recv())

    def wait_send(self):
        self.each(lambda peer: self.copy(peer, self.me).wait_send())


def split_sum(total):
    high = total.astype(BF16).astype(F32)
    lane = lax.broadcasted_iota(jnp.int32, (total.shape[0], 128), 1)
    return jnp.where(lane == 0, high, jnp.where(lane == 1, total - high, 0.0)).astype(BF16)


def loss_row(value):
    row, lane = iotas(32, KVW)
    spread = jnp.full((32, KVW), value, F32)
    high = spread.astype(BF16).astype(F32)
    middle = (spread - high).astype(BF16).astype(F32)
    low = spread - high - middle
    picked = jnp.where(lane == 0, high, jnp.where(lane == 1, middle, jnp.where(lane == 2, low, 0.0)))
    return jnp.where(row == LOSS_ROW, picked, 0.0)


def loss_of(block):
    row, _ = iotas(32, KVW)
    return jnp.sum(jnp.where(row == LOSS_ROW, block, 0.0))


def ring_sum(out, at, mine, other, width):
    mine, other = mine.astype(F32), other.astype(F32)
    total = mine + other
    out[at, :, :width] = total[:, :width].astype(BF16)
    if out.shape[2] > width:
        out[at, :, width:] = split_sum(jnp.sum(total[:, width:], axis=1, keepdims=True))


def transpose_runs(a):
    lane = lax.broadcasted_iota(jnp.int32, a[0].shape, 1)
    for step in (4, 2, 1):
        upper = (lane & (16 * step)) != 0
        new = list(a)
        for j in range(8):
            if j & step == 0:
                low, high = a[j], a[j + step]
                new[j] = jnp.where(upper, pltpu.roll(high, 16 * step, 1), low)
                new[j + step] = jnp.where(upper, high, pltpu.roll(low, 128 - 16 * step, 1))
        a = new
    return a


def one_hot(hit):
    return jnp.where(hit, 1.0, 0.0).astype(BF16)


def iotas(*shape):
    return [lax.broadcasted_iota(jnp.int32, shape, axis) for axis in range(2)]


def kernel(
    total_count,
    names,
    x_ref,
    codes_ref,
    scales_ref,
    residt_ref,
    gain_ref,
    proj_ref,
    routes_ref,
    stu_ref,
    seg_ref,
    vw_ref,
    q_ref,
    k_ref,
    loss_ref,
    grad_ref,
    *scratch,
):
    m = SimpleNamespace(**dict(zip(names, scratch)))
    flow = Flow()

    d, f, t = lax.axis_index("dp"), lax.axis_index("fsdp"), lax.axis_index("tensor")
    zh, c = lax.div(t, 2), lax.rem(t, 2)
    other = 1 - c
    sib = t + 1 - 2 * c
    zp, zm = lax.rem(t + 2, N), lax.rem(t + 6, N)
    fz = f + 1 - 2 * lax.rem(f, 2)
    xp, xm = lax.rem(f + 2, N), lax.rem(f + 6, N)
    xpz, xmz = xp + 1 - 2 * lax.rem(xp, 2), xm + 1 - 2 * lax.rem(xm, 2)
    xf = lax.rem(f + 4, N)
    xfz = xf + 1 - 2 * lax.rem(xf, 2)

    barrier = pltpu.get_barrier_semaphore()

    def greet(step, carry):
        for axis, me in (("tensor", t), ("fsdp", f), ("dp", d)):
            pl.semaphore_signal(
                barrier, inc=1, device_id={axis: lax.rem(me + step, N)}, device_id_type=MESH
            )
        return carry

    lax.fori_loop(1, N, greet, 0)

    zl, xi = lax.rem(f, 2), lax.div(f, 2)
    inputs = [
        (codes_ref, m.codes),
        (x_ref, m.x),
        (stu_ref.at[pl.ds(0, LEAD)], m.stu),
        (proj_ref, m.proj.at[c, zl, xi]),
        (residt_ref, m.residt),
        (q_ref.at[pl.ds(0, LEAD)], m.q),
        (k_ref.at[pl.ds(0, LEAD)], m.k),
        (routes_ref, m.routes),
    ]
    inputs = [pltpu.make_async_copy(src, dst, m.in_sem.at[i]) for i, (src, dst) in enumerate(inputs)]
    codes_in, x_in, stu_in, proj_in, resid_in, q_in, k_in, routes_in = inputs
    for copy in inputs:
        copy.start()

    row, col = iotas(512, 512)
    own_order = ((row >> 4) & 7) * 64 + (row & 15) * 4 + (row >> 7)
    m.spread[...] = one_hot(own_order == col)

    scales = jnp.concatenate([scales_ref[...].astype(F32), jnp.zeros((4, HT), F32)], axis=0)
    scales = jnp.concatenate([scales[:, j * 512 : (j + 1) * 512] for j in range(8)], axis=0)
    scales = dot(scales.astype(BF16), m.spread[...], ((1,), (1,)))
    for level in range(4):
        lanes = slice(level * 128, (level + 1) * 128)
        for j, piece in enumerate(transpose_runs([scales[8 * j : 8 * j + 8, lanes] for j in range(8)])):
            m.scp[8 * j : 8 * j + 8, lanes] = piece

    def shuffle(i, carry):
        at = pl.ds(pl.multiple_of(i * 32, 32), 32)
        far_at = pl.ds(pl.multiple_of(i * 32 + 256, 32), 32)
        words = []
        for j in range(8):
            lanes = slice(j * 128, (j + 1) * 128)
            words.append(m.codes[at, lanes] | (m.codes[far_at, lanes] << 16))
        for j, piece in enumerate(transpose_runs(words)):
            m.perm[j, at, :] = piece
        return carry

    def slots(ref):
        return lambda slot: ref.at[slot]

    def block(owner):
        return m.proj.at[c, lax.rem(owner, 2), lax.div(owner, 2)]

    def half_block(owner, half):
        return m.proj.at[c, lax.rem(owner, 2), lax.div(owner, 2), pl.ds(32 * half, 32)]

    def pass_on(i, owner, half=None, src=None, **device):
        dst = block(owner) if half is None else half_block(owner, half)
        return remote(dst if src is None else src, dst, m.p_s.at[i], m.p_r.at[owner, half or 0], **device)

    to_z = pass_on(0, f, src=proj_ref, fsdp=fz)
    from_z = pass_on(0, fz, fsdp=fz)
    near_same = [pass_on(1, owner, fsdp=fz) for owner in (xm, xp)]
    near_other = [pass_on(1, owner, fsdp=fz) for owner in (xmz, xpz)]
    far_same = [pass_on(1, xf, half, fsdp=fz) for half in range(2)]
    far_other = [pass_on(1, xfz, half, fsdp=fz) for half in range(2)]
    def block_to_sibling(owner, slot):
        dst = m.proj.at[slot, lax.rem(owner, 2), lax.div(owner, 2)]
        return remote(block(owner), dst, m.psib_s.at[owner], m.psib_r.at[owner], tensor=sib)

    owners = (f, xm, xp, xf, fz, xmz, xpz, xfz)
    proj_here = [block_to_sibling(owner, other) for owner in owners]

    def share(*places):
        flow.start(*(block_to_sibling(owners[i], c) for i in places), due=[proj_here[i] for i in places])

    value_rows = Exchange("tensor", t, lambda peer: m.vwp, slots(m.vw), m.vwz_s, m.vwz_r)
    value_slices = Exchange("dp", d, lambda peer: m.vw.at[d], slots(m.vw), m.vwy_s, m.vwy_r)

    class ValueRows:
        def start(self):
            @pl.when(t == d)
            def _():
                m.vw[d] = m.vwp[...]
                value_rows.start()

        def wait_recv(self):
            @pl.when(t != d)
            def _():
                value_rows.copy(d, d).wait_recv()

        def wait_send(self):
            @pl.when(t == d)
            def _():
                value_rows.wait_send()

    sent_rows = ValueRows()
    row, col = iotas(32, 28)
    m.vwp[...] = dot(one_hot(row == col), vw_ref[...]).astype(BF16)

    pl.semaphore_wait(barrier, 3 * (N - 1))
    flow.start(to_z, due=[from_z])
    flow.start(pass_on(1, f, src=proj_ref, fsdp=xp), pass_on(2, f, src=proj_ref, fsdp=xm), due=near_same)
    flow.start(sent_rows, due=[sent_rows])

    codes_in.wait()
    lax.fori_loop(0, 8, shuffle, 0, unroll=4)
    x_in.wait()
    for b in range(4):
        m.xb[0, b] = m.x[b, c]
        m.xb[1, b] = m.x[b, other]

    def partial(r):
        z = lax.rem(zh + r, ZH)

        def dequantize(s, carry):
            slice_at = 2 * z + s
            sc = m.scp[pl.ds(pl.multiple_of(slice_at * 8, 8), 8), :]
            for g in range(4):
                at = slice(g * GROUP, (g + 1) * GROUP)
                words = m.perm[slice_at, g % 2 * GROUP : (g % 2 + 1) * GROUP, :]
                for level in range(4):
                    value = lax.shift_right_logical(words, g // 2 * 16 + 4 * level) & 15
                    value = value.astype(F32) - 8.0
                    value = value * sc[g : g + 1, level * 128 : (level + 1) * 128]
                    lanes = pl.ds(pl.multiple_of(s * 512 + level * 128, 128), 128)
                    m.wbuf[at, lanes] = value.astype(BF16)
            return carry

        lax.fori_loop(0, 2, dequantize, 0)
        rows = m.xb[...].reshape(256, 512)
        for s in range(2):
            lanes = slice(s * 512, (s + 1) * 512)
            acc = dot(rows, m.wbuf[:, lanes]).astype(BF16)
            acc = dot(acc, m.spread[...]).astype(BF16)
            m.part[r, :, lanes] = acc[0:128]
            m.half_out[r, :, lanes] = acc[128:256]

    def to_sibling(i, src, dst):
        return remote(src, dst, m.sib_s.at[i], m.sib_r.at[i], tensor=sib)

    halves = [to_sibling(r, m.half_out.at[r], m.half_in.at[r]) for r in range(ZH)]
    resid_there = to_sibling(4, m.resid.at[:, other], m.resb.at[c])
    resid_here = to_sibling(4, m.resid.at[:, other], m.resb.at[other])
    gain_there = to_sibling(5, m.gainb.at[c], m.gainb.at[c])
    gain_here = to_sibling(5, m.gainb.at[c], m.gainb.at[other])

    def add_half(r):
        flow.wait(halves[r])
        m.part[r] = (m.part[r].astype(F32) + m.half_in[r].astype(F32)).astype(BF16)

    students = Exchange("fsdp", f, slots(m.stus), slots(m.sb), m.stu_s, m.stu_r)
    value_parts = Exchange("fsdp", f, slots(m.pvs), slots(m.pvr), m.pv_s, m.pv_r)
    targets = [
        Exchange("dp", d, slots(m.osend0), slots(m.trecv0), m.t5a_s, m.t5a_r),
        Exchange("dp", d, slots(m.osend1), slots(m.trecv1), m.t5b_s, m.t5b_r),
    ]
    grads1 = Exchange("fsdp", f, lambda peer: m.g1.at[f], slots(m.g1), m.g1_s, m.g1_r)
    losses = Exchange("fsdp", f, lambda peer: m.lost.at[f], slots(m.lost), m.loss_s, m.loss_r)
    grads2 = Exchange("tensor", t, slots(m.g2s), slots(m.g2r), m.g2_s, m.g2_r)
    grads3 = Exchange("dp", d, lambda peer: m.g3.at[d], slots(m.g3), m.g3_s, m.g3_r)

    def ring(src, name, half):
        relay, near, added, summed, send, recv = (
            getattr(m, f"{name}_{end}") for end in ("relay", "near", "added", "summed", "s", "r")
        )
        low, high = pl.ds(0, half), pl.ds(half, half)
        far = [
            remote(src(2, low), relay.at[0], send.at[0], recv.at[0], tensor=zp),
            remote(src(2, high), relay.at[1], send.at[1], recv.at[1], tensor=zm),
        ]
        direct = [
            remote(src(1, high), near.at[0], send.at[2], recv.at[2], tensor=zp),
            remote(src(3, low), near.at[1], send.at[3], recv.at[3], tensor=zm),
        ]
        sums = [
            remote(added.at[0], summed.at[0], send.at[4], recv.at[4], tensor=zp),
            remote(added.at[1], summed.at[1], send.at[5], recv.at[5], tensor=zm),
        ]
        return far, direct, sums

    far, direct, sums = ring(lambda r, rows: m.part.at[r, rows], "t1", 64)
    partial(2)
    flow.start(halves[2], due=[halves[2]])
    partial(1)
    flow.start(halves[1], due=[halves[1]])
    add_half(2)
    flow.start(*far, due=far)
    flow.wait(from_z)
    flow.start(pass_on(5, fz, fsdp=xp), pass_on(6, fz, fsdp=xm), due=near_other)
    flow.wait(*near_same)
    flow.start(pass_on(3, xm, 0, fsdp=xp), pass_on(4, xp, 1, fsdp=xm), due=far_same)
    partial(3)
    flow.start(halves[3], due=[halves[3]])
    add_half(1)
    flow.start(direct[0], due=direct[:1])
    proj_in.wait()
    partial(0)
    flow.start(halves[0], due=[halves[0]])
    add_half(3)
    flow.start(direct[1], due=direct[1:])
    flow.wait(sent_rows)
    flow.start(value_slices, due=[value_slices])
    share(0, 1, 2, 4)

    resid_in.wait()
    row, col = iotas(512, 512)
    m.resid[...] = dot(m.residt[...], one_hot(row == col), ((0,), (0,))).astype(BF16).reshape(4, 2, 32, 512)
    for b in range(4):
        m.resb[c, b] = m.resid[b, c]
    row, col = iotas(64, 512)
    gain = dot(gain_ref[...], one_hot((col & 63) == row))
    row, col = iotas(8, 512)
    gain = jnp.sum(jnp.where((col >> 6) == row, gain, 0.0), axis=0, keepdims=True)
    m.gainb[c] = jnp.broadcast_to(gain, (8, 512))
    flow.start(resid_there, gain_there, due=[resid_here, gain_here])
    add_half(0)

    flow.wait(*near_other)
    flow.start(pass_on(7, xmz, 0, fsdp=xp), pass_on(8, xpz, 1, fsdp=xm), due=far_other)
    share(5, 6)
    flow.wait(far[0])
    ring_sum(m.t1_added, 0, m.part[1, 0:64], m.t1_relay[0], 1024)
    flow.start(sums[0], due=sums[:1])
    flow.wait(far[1])
    ring_sum(m.t1_added, 1, m.part[3, 64:128], m.t1_relay[1], 1024)
    flow.start(sums[1], due=sums[1:])

    stu_in.wait()
    row, col = iotas(896, 1024)
    pad = one_hot(((col >> 5) * 28 + (col & 31) == row) & ((col & 31) < 28))
    for j in range(2):
        padded = dot(m.stu[:, j * 896 : (j + 1) * 896], pad).astype(BF16)
        for i in range(4):
            m.stus[4 * j + i] = padded[:, i * KVW : (i + 1) * KVW]
    m.sb[f] = m.stus[f]

    places = jnp.broadcast_to(seg_ref[0:1, 0:128].astype(F32), (128, 128))
    same = places == jnp.transpose(places)
    row, col = iotas(128, 128)
    allow = jnp.where(same & (row >= col), 1.0, 0.0)[:LEAD, :LEAD]
    allow = jnp.concatenate([allow] * 7, axis=0)
    q_in.wait()
    k_in.wait()
    for g in range(2):
        heads = [m.q[:, (g * 7 + h) * HEAD : (g * 7 + h + 1) * HEAD] for h in range(7)]
        scores = dot(jnp.concatenate(heads, axis=0), m.k[:, g * HEAD : (g + 1) * HEAD], ((1,), (1,)))
        scores = jnp.where(allow > 0.0, scores * HEAD ** (-0.5), -1e30)
        weights = jnp.exp(scores - jnp.max(scores, axis=1, keepdims=True))
        probs = weights / jnp.sum(weights, axis=1, keepdims=True)
        m.probs[g] = probs.astype(BF16)
        m.probs_t[g] = jnp.transpose(probs).astype(BF16)

    routes_in.wait()
    row, col = iotas(64, 32)
    place = ((d * N + f) * N + t) * 4
    wanted = jnp.full((64, 32), -1, jnp.int32)
    for j in range(4):
        wanted = jnp.where((col >> 3) == j, m.routes[place + j], wanted)
    select = one_hot(((row >> 3) == wanted) & ((row & 7) == (col & 7)))
    lead = lax.broadcasted_iota(jnp.int32, (LEAD, HEAD), 0) >> 3
    mask = jnp.zeros((LEAD, HEAD), F32)
    for source in range(N):
        for j in range(4):
            hit = m.routes[((source * N + f) * N + t) * 4 + j] == d
            mask = jnp.where(lead == source, jnp.maximum(mask, jnp.where(hit, 1.0, 0.0)), mask)

    flow.wait(*far_same)
    share(3)
    flow.wait(*far_other)
    share(7)
    flow.wait(*direct, *sums, resid_here, gain_here)
    flow.start(students, due=[students])

    lower = m.part[0, 0:64].astype(F32) + m.t1_summed[0].astype(F32) + m.t1_near[1].astype(F32)
    upper = m.part[0, 64:128].astype(F32) + m.t1_near[0].astype(F32) + m.t1_summed[1].astype(F32)
    out = jnp.concatenate([lower, upper], axis=0)
    power = jnp.zeros((128, 1), F32)
    scaled = []
    for s in range(2):
        hidden = out[:, s * 512 : (s + 1) * 512] + m.resb[s].reshape(128, 512).astype(F32)
        power = power + jnp.sum(hidden * hidden, axis=1, keepdims=True)
        scaled.append((hidden * m.gainb[s, 0:1, :]).astype(BF16))
    m.pbuf0[:, :, CHUNKS[0] :] = split_sum(power).reshape(ZH, 32, 128)
    flow.wait(*proj_here)

    def ahead(pbuf):
        return lambda r, rows: pbuf.at[lax.rem(zh + r, ZH), rows]

    rings = [ring(ahead(m.pbuf0), "t4a", 16), ring(ahead(m.pbuf1), "t4b", 16)]
    pbufs = (m.pbuf0, m.pbuf1)
    for i in range(2):
        for j in range(CHUNKS[i] // 256):
            lanes = slice(j * 256, (j + 1) * 256)
            from_lanes = slice(i * CHUNKS[0] + j * 256, i * CHUNKS[0] + (j + 1) * 256)
            acc = jnp.zeros((128, 256), F32)
            for s in range(2):
                rows = [m.proj[s, owner % 2, owner // 2, :, from_lanes] for owner in range(8)]
                acc = acc + dot(scaled[s], jnp.concatenate(rows, axis=0))
            pbufs[i][:, :, lanes] = acc.astype(BF16).reshape(ZH, 32, 256)
        flow.start(*rings[i][0], *rings[i][1], due=rings[i][0] + rings[i][1])
    for i, name in enumerate(("t4a", "t4b")):
        far4, direct4, sums4 = rings[i]
        relay, added = getattr(m, f"{name}_relay"), getattr(m, f"{name}_added")
        for way, r in enumerate((1, 3)):
            flow.wait(far4[way])
            mine = pbufs[i][lax.rem(zh + r, ZH), 16 * way : 16 * way + 16]
            ring_sum(added, way, mine, relay[way], CHUNKS[i])
            flow.start(sums4[way], due=[sums4[way]])

    flow.wait(students, value_slices)
    rows_of_value = m.vw[...].reshape(8 * 32, KVW)
    value_part = dot(m.sb[...].reshape(8 * LEAD, KVW), rows_of_value)
    m.pvs[...] = value_part.reshape(8, LEAD, KVW).astype(BF16)
    m.pvr[f] = m.pvs[f]
    m.sb_t[...] = jnp.transpose(m.sb[...].reshape(8 * LEAD, KVW).astype(F32)).astype(BF16)

    row_scale = None
    for i, name in enumerate(("t4a", "t4b")):
        _, direct4, sums4 = rings[i]
        flow.wait(*direct4, *sums4)
        near, summed = getattr(m, f"{name}_near"), getattr(m, f"{name}_summed")
        own = pbufs[i][zh].astype(F32)
        lower = own[0:16] + summed[0].astype(F32) + near[1].astype(F32)
        upper = own[16:32] + near[0].astype(F32) + summed[1].astype(F32)
        total = jnp.concatenate([lower, upper], axis=0)
        if i == 0:
            power = jnp.sum(total[:, CHUNKS[0] :], axis=1, keepdims=True)
            row_scale = lax.rsqrt(power / HT + EPS)
        routed = dot(select, (total[:, : CHUNKS[i]] * row_scale).astype(BF16))
        half = CHUNKS[i] // 2
        osend, trecv = getattr(m, f"osend{i}"), getattr(m, f"trecv{i}")
        osend[...] = jnp.concatenate(
            [routed[:, :half].reshape(8, 8, half), routed[:, half:].reshape(8, 8, half)], axis=1
        ).astype(BF16)
        trecv[d] = osend[d]
        flow.start(targets[i], due=[targets[i]])
    flow.start(value_parts, due=[value_parts])
    flow.wait(value_parts)
    values = m.pvr[0].astype(F32)
    for j in range(1, 8):
        values = values + m.pvr[j].astype(F32)
    values = values.astype(BF16)
    attended = [dot(m.probs[g], values[:, g * HEAD : (g + 1) * HEAD]) for g in range(2)]

    lost = jnp.zeros((LEAD, HEAD), F32)
    pieces_of = ([], [])
    for i in range(2):
        flow.wait(targets[i])
        received = getattr(m, f"trecv{i}")[...].astype(F32)
        per_half = CHUNKS[i] // 2 // HEAD
        for j in range(2 * per_half):
            at, lane = j // per_half * 8, j % per_half * HEAD
            wanted = received[:, at : at + 8, lane : lane + HEAD].reshape(LEAD, HEAD)
            head = i * (CHUNKS[0] // HEAD) + j
            g, h = head // 7, head % 7
            diff = attended[g][h * LEAD : (h + 1) * LEAD] - wanted
            masked = diff * mask
            lost = lost + masked * diff
            pieces_of[g].append((2.0 * masked / QW).astype(BF16))
    for g in range(2):
        grad = dot(m.probs_t[g], jnp.concatenate(pieces_of[g], axis=0))
        m.g1[f, :, g * HEAD : (g + 1) * HEAD] = grad.astype(BF16)
    flow.start(grads1, due=[grads1])
    lost = lost.reshape(8, 8, 128).sum(axis=0)
    m.lost[f] = lost
    flow.start(losses, due=[losses])
    flow.wait(grads1)
    grad = dot(m.sb_t[...], m.g1[...].reshape(8 * LEAD, KVW))
    flow.wait(losses)
    tail = loss_row(jnp.sum(m.lost[...]))
    for j in range(N):
        m.g2s[j] = (grad[32 * j : 32 * j + 32] + tail).astype(BF16)
    m.g2r[t] = m.g2s[t]
    flow.start(grads2, due=[grads2])
    flow.wait(grads2)
    row, _ = iotas(32, KVW)
    total = jnp.sum(m.g2r[...].astype(F32), axis=0)
    m.g3[d] = jnp.where(row < LOSS_ROW, total, loss_row(loss_of(total))).astype(BF16)
    flow.start(grads3, due=[grads3])
    flow.wait(grads3)
    total = jnp.sum(m.g3[...].astype(F32), axis=0)
    grad_ref[...] = total[0:LOSS_ROW]
    loss_ref[0, 0] = loss_of(total) / total_count
    flow.finish()


def local(
    teacher_in,
    codes,
    scales,
    teacher_resid,
    teacher_gain,
    projector,
    routes,
    student_in,
    queries,
    keys,
    segments,
    value_weight,
):
    spec = scratch_spec()
    vmem = pl.BlockSpec(memory_space=pltpu.VMEM)
    smem = pl.BlockSpec(memory_space=pltpu.SMEM)
    hbm = pl.BlockSpec(memory_space=pltpu.HBM)
    loss, grad = pl.pallas_call(
        functools.partial(kernel, float(16384 * QW), tuple(spec)),
        out_shape=(
            jax.ShapeDtypeStruct((1, 1), F32),
            jax.ShapeDtypeStruct((28, KVW), F32),
        ),
        in_specs=[hbm, hbm, vmem, hbm, vmem, hbm, hbm, hbm, vmem, vmem, hbm, hbm],
        out_specs=(smem, vmem),
        scratch_shapes=list(spec.values()),
        compiler_params=pltpu.CompilerParams(
            collective_id=0, has_side_effects=True, vmem_limit_bytes=56 * 1024 * 1024
        ),
        name="distill",
    )(
        teacher_in.reshape(4, 2, 32, 512),
        codes,
        scales,
        teacher_resid.transpose(1, 2, 0).reshape(512, 256),
        teacher_gain,
        projector.reshape(64, QW),
        routes.reshape(2048),
        student_in,
        segments.reshape(1, 256),
        value_weight,
        queries,
        keys,
    )
    return loss[0, 0], grad


def solution(mesh):
    return jax.shard_map(
        local,
        mesh=mesh,
        in_specs=(
            P(("dp", "fsdp"), "tensor"),
            P("tensor", None),
            P("tensor", None),
            P(("dp", "fsdp"), None, "tensor"),
            P(None, "tensor"),
            P("fsdp", "tensor", None),
            P(),
            P(("dp", "fsdp", "tensor"), None),
            P(("dp", "fsdp", "tensor"), None),
            P(("dp", "fsdp", "tensor"), None),
            P(("dp", "fsdp", "tensor")),
            P(("fsdp", "tensor"), None),
        ),
        out_specs=(P(), P(("fsdp", "tensor"), None)),
        check_vma=False,
    )
```

```python
import functools
from types import SimpleNamespace

import jax
import jax.numpy as jnp
from jax import lax
from jax.experimental import pallas as pl
from jax.experimental.pallas import tpu as pltpu
from jax.sharding import PartitionSpec as P

HT = 4096
GROUP = 128
HEAD = 128
EPS = 1e-06
F32, BF16 = jnp.float32, jnp.bfloat16
MESH = pl.DeviceIdType.MESH

N = 8
ZH = 4
LEAD = 64
QW = 1792
KVW = 256
CHUNKS = (1024, 768)
WIDTHS = (1024 + 128, 768)
LOSS_ROW = 28


def ring_buffers(name, rows, width):
    block, sems = pltpu.VMEM((2, rows, width), BF16), pltpu.SemaphoreType.DMA((6,))
    spec = {f"{name}_{part}": block for part in ("relay", "near", "added", "summed")}
    return spec | {f"{name}_s": sems, f"{name}_r": sems}


def scratch_spec():
    dma, vmem = pltpu.SemaphoreType.DMA, pltpu.VMEM
    return dict(
        codes=vmem((512, 1024), jnp.int32),
        routes=pltpu.SMEM((2048,), jnp.int32),
        x=vmem((4, 2, 32, 512), BF16),
        xb=vmem((2, 4, 32, 512), BF16),
        stu=vmem((LEAD, QW), BF16),
        stus=vmem((8, LEAD, KVW), BF16),
        residt=vmem((512, 256), BF16),
        resid=vmem((4, 2, 32, 512), BF16),
        resb=vmem((2, 4, 32, 512), BF16),
        gainb=vmem((2, 8, 512), F32),
        vwp=vmem((32, KVW), BF16),
        vw=vmem((8, 32, KVW), BF16),
        perm=vmem((8, 256, 128), jnp.int32),
        scp=vmem((64, 512), F32),
        spread=vmem((512, 512), BF16),
        wbuf=vmem((512, 1024), BF16),
        part=vmem((ZH, 128, 1024), BF16),
        half_out=vmem((ZH, 128, 1024), BF16),
        half_in=vmem((ZH, 128, 1024), BF16),
        proj=vmem((2, 2, 4, 64, QW), BF16),
        q=vmem((LEAD, QW), BF16),
        k=vmem((LEAD, KVW), BF16),
        sb=vmem((8, LEAD, KVW), BF16),
        pvs=vmem((8, LEAD, KVW), BF16),
        pvr=vmem((8, LEAD, KVW), BF16),
        probs=vmem((2, 7 * LEAD, LEAD), BF16),
        probs_t=vmem((2, LEAD, 7 * LEAD), BF16),
        sb_t=vmem((KVW, 8 * LEAD), BF16),
        g1=vmem((8, LEAD, KVW), BF16),
        lost=vmem((8, 8, 128), F32),
        g2s=vmem((8, 32, KVW), BF16),
        g2r=vmem((8, 32, KVW), BF16),
        g3=vmem((8, 32, KVW), BF16),
        **ring_buffers("t1", 64, 1024),
        **{f"pbuf{i}": vmem((ZH, 32, width), BF16) for i, width in enumerate(WIDTHS)},
        **ring_buffers("t4a", 16, WIDTHS[0]),
        **ring_buffers("t4b", 16, WIDTHS[1]),
        **{f"osend{i}": vmem((8, 16, width // 2), BF16) for i, width in enumerate(CHUNKS)},
        **{f"trecv{i}": vmem((8, 16, width // 2), BF16) for i, width in enumerate(CHUNKS)},
        in_sem=dma((8,)),
        sib_s=dma((6,)),
        sib_r=dma((6,)),
        p_s=dma((9,)),
        p_r=dma((8, 2)),
        psib_s=dma((8,)),
        psib_r=dma((8,)),
        **{
            name + end: dma((8,))
            for name in ("stu", "vwz", "vwy", "pv", "t5a", "t5b", "g1", "loss", "g2", "g3")
            for end in ("_s", "_r")
        },
    )


def dot(a, b, dims=((1,), (0,))):
    return lax.dot_general(a, b, (dims, ((), ())), preferred_element_type=F32)


def remote(src, dst, send, recv, **device):
    return pltpu.make_async_remote_copy(
        src_ref=src,
        dst_ref=dst,
        send_sem=send,
        recv_sem=recv,
        device_id=device,
        device_id_type=MESH,
    )


class Flow:
    def __init__(self):
        self.sent, self.due = [], []

    def start(self, *copies, due=()):
        for copy in copies:
            copy.start()
        self.sent += copies
        self.due += list(due)

    def wait(self, *copies):
        for copy in copies:
            copy.wait_recv()
            self.due = [left for left in self.due if left is not copy]

    def finish(self):
        for copy in list(self.due):
            self.wait(copy)
        for copy in self.sent:
            copy.wait_send()


class Exchange:
    def __init__(self, axis, me, src, dst, send, recv):
        self.axis, self.me, self.src, self.dst = axis, me, src, dst
        self.send, self.recv = send, recv

    def each(self, act):
        def body(step, carry):
            act(lax.rem(self.me + step, N))
            return carry

        lax.fori_loop(1, N, body, 0)

    def copy(self, peer, slot):
        return remote(
            self.src(peer),
            self.dst(slot),
            self.send.at[peer],
            self.recv.at[slot],
            **{self.axis: peer},
        )

    def start(self):
        self.each(lambda peer: self.copy(peer, self.me).start())

    def wait_recv(self):
        self.each(lambda peer: self.copy(peer, peer).wait_recv())

    def wait_send(self):
        self.each(lambda peer: self.copy(peer, self.me).wait_send())


def split_sum(total):
    high = total.astype(BF16).astype(F32)
    lane = lax.broadcasted_iota(jnp.int32, (total.shape[0], 128), 1)
    return jnp.where(lane == 0, high, jnp.where(lane == 1, total - high, 0.0)).astype(BF16)


def loss_row(value):
    row, lane = iotas(32, KVW)
    spread = jnp.full((32, KVW), value, F32)
    high = spread.astype(BF16).astype(F32)
    middle = (spread - high).astype(BF16).astype(F32)
    low = spread - high - middle
    picked = jnp.where(lane == 0, high, jnp.where(lane == 1, middle, jnp.where(lane == 2, low, 0.0)))
    return jnp.where(row == LOSS_ROW, picked, 0.0)


def loss_of(block):
    row, _ = iotas(32, KVW)
    return jnp.sum(jnp.where(row == LOSS_ROW, block, 0.0))


def ring_sum(out, at, mine, other, width):
    mine, other = mine.astype(F32), other.astype(F32)
    total = mine + other
    out[at, :, :width] = total[:, :width].astype(BF16)
    if out.shape[2] > width:
        out[at, :, width:] = split_sum(jnp.sum(total[:, width:], axis=1, keepdims=True))


def transpose_runs(a):
    lane = lax.broadcasted_iota(jnp.int32, a[0].shape, 1)
    for step in (4, 2, 1):
        upper = (lane & (16 * step)) != 0
        new = list(a)
        for j in range(8):
            if j & step == 0:
                low, high = a[j], a[j + step]
                new[j] = jnp.where(upper, pltpu.roll(high, 16 * step, 1), low)
                new[j + step] = jnp.where(upper, high, pltpu.roll(low, 128 - 16 * step, 1))
        a = new
    return a


def one_hot(hit):
    return jnp.where(hit, 1.0, 0.0).astype(BF16)


def iotas(*shape):
    return [lax.broadcasted_iota(jnp.int32, shape, axis) for axis in range(2)]


def kernel(
    total_count,
    names,
    x_ref,
    codes_ref,
    scales_ref,
    residt_ref,
    gain_ref,
    proj_ref,
    routes_ref,
    stu_ref,
    seg_ref,
    vw_ref,
    q_ref,
    k_ref,
    loss_ref,
    grad_ref,
    *scratch,
):
    m = SimpleNamespace(**dict(zip(names, scratch)))
    flow = Flow()

    d, f, t = lax.axis_index("dp"), lax.axis_index("fsdp"), lax.axis_index("tensor")
    zh, c = lax.div(t, 2), lax.rem(t, 2)
    other = 1 - c
    sib = t + 1 - 2 * c
    zp, zm = lax.rem(t + 2, N), lax.rem(t + 6, N)
    fz = f + 1 - 2 * lax.rem(f, 2)
    xp, xm = lax.rem(f + 2, N), lax.rem(f + 6, N)
    xpz, xmz = xp + 1 - 2 * lax.rem(xp, 2), xm + 1 - 2 * lax.rem(xm, 2)
    xf = lax.rem(f + 4, N)
    xfz = xf + 1 - 2 * lax.rem(xf, 2)

    barrier = pltpu.get_barrier_semaphore()

    def greet(step, carry):
        for axis, me in (("tensor", t), ("fsdp", f), ("dp", d)):
            pl.semaphore_signal(
                barrier, inc=1, device_id={axis: lax.rem(me + step, N)}, device_id_type=MESH
            )
        return carry

    lax.fori_loop(1, N, greet, 0)

    zl, xi = lax.rem(f, 2), lax.div(f, 2)
    inputs = [
        (codes_ref, m.codes),
        (x_ref, m.x),
        (stu_ref.at[pl.ds(0, LEAD)], m.stu),
        (proj_ref, m.proj.at[c, zl, xi]),
        (residt_ref, m.residt),
        (q_ref.at[pl.ds(0, LEAD)], m.q),
        (k_ref.at[pl.ds(0, LEAD)], m.k),
        (routes_ref, m.routes),
    ]
    inputs = [pltpu.make_async_copy(src, dst, m.in_sem.at[i]) for i, (src, dst) in enumerate(inputs)]
    codes_in, x_in, stu_in, proj_in, resid_in, q_in, k_in, routes_in = inputs
    for copy in inputs:
        copy.start()

    row, col = iotas(512, 512)
    own_order = ((row >> 4) & 7) * 64 + (row & 15) * 4 + (row >> 7)
    m.spread[...] = one_hot(own_order == col)

    scales = jnp.concatenate([scales_ref[...].astype(F32), jnp.zeros((4, HT), F32)], axis=0)
    scales = jnp.concatenate([scales[:, j * 512 : (j + 1) * 512] for j in range(8)], axis=0)
    scales = dot(scales.astype(BF16), m.spread[...], ((1,), (1,)))
    for level in range(4):
        lanes = slice(level * 128, (level + 1) * 128)
        for j, piece in enumerate(transpose_runs([scales[8 * j : 8 * j + 8, lanes] for j in range(8)])):
            m.scp[8 * j : 8 * j + 8, lanes] = piece

    def shuffle(i, carry):
        at = pl.ds(pl.multiple_of(i * 32, 32), 32)
        far_at = pl.ds(pl.multiple_of(i * 32 + 256, 32), 32)
        words = []
        for j in range(8):
            lanes = slice(j * 128, (j + 1) * 128)
            words.append(m.codes[at, lanes] | (m.codes[far_at, lanes] << 16))
        for j, piece in enumerate(transpose_runs(words)):
            m.perm[j, at, :] = piece
        return carry

    def slots(ref):
        return lambda slot: ref.at[slot]

    def block(owner):
        return m.proj.at[c, lax.rem(owner, 2), lax.div(owner, 2)]

    def half_block(owner, half):
        return m.proj.at[c, lax.rem(owner, 2), lax.div(owner, 2), pl.ds(32 * half, 32)]

    def pass_on(i, owner, half=None, src=None, **device):
        dst = block(owner) if half is None else half_block(owner, half)
        return remote(dst if src is None else src, dst, m.p_s.at[i], m.p_r.at[owner, half or 0], **device)

    to_z = pass_on(0, f, src=proj_ref, fsdp=fz)
    from_z = pass_on(0, fz, fsdp=fz)
    near_same = [pass_on(1, owner, fsdp=fz) for owner in (xm, xp)]
    near_other = [pass_on(1, owner, fsdp=fz) for owner in (xmz, xpz)]
    far_same = [pass_on(1, xf, half, fsdp=fz) for half in range(2)]
    far_other = [pass_on(1, xfz, half, fsdp=fz) for half in range(2)]
    def block_to_sibling(owner, slot):
        dst = m.proj.at[slot, lax.rem(owner, 2), lax.div(owner, 2)]
        return remote(block(owner), dst, m.psib_s.at[owner], m.psib_r.at[owner], tensor=sib)

    owners = (f, xm, xp, xf, fz, xmz, xpz, xfz)
    proj_here = [block_to_sibling(owner, other) for owner in owners]

    def share(*places):
        flow.start(*(block_to_sibling(owners[i], c) for i in places), due=[proj_here[i] for i in places])

    value_rows = Exchange("tensor", t, lambda peer: m.vwp, slots(m.vw), m.vwz_s, m.vwz_r)
    value_slices = Exchange("dp", d, lambda peer: m.vw.at[d], slots(m.vw), m.vwy_s, m.vwy_r)

    class ValueRows:
        def start(self):
            @pl.when(t == d)
            def _():
                m.vw[d] = m.vwp[...]
                value_rows.start()

        def wait_recv(self):
            @pl.when(t != d)
            def _():
                value_rows.copy(d, d).wait_recv()

        def wait_send(self):
            @pl.when(t == d)
            def _():
                value_rows.wait_send()

    sent_rows = ValueRows()
    row, col = iotas(32, 28)
    m.vwp[...] = dot(one_hot(row == col), vw_ref[...]).astype(BF16)

    pl.semaphore_wait(barrier, 3 * (N - 1))
    flow.start(to_z, due=[from_z])
    flow.start(pass_on(1, f, src=proj_ref, fsdp=xp), pass_on(2, f, src=proj_ref, fsdp=xm), due=near_same)
    flow.start(sent_rows, due=[sent_rows])

    codes_in.wait()
    lax.fori_loop(0, 8, shuffle, 0, unroll=4)
    x_in.wait()
    for b in range(4):
        m.xb[0, b] = m.x[b, c]
        m.xb[1, b] = m.x[b, other]

    def partial(r):
        z = lax.rem(zh + r, ZH)

        def dequantize(s, carry):
            slice_at = 2 * z + s
            sc = m.scp[pl.ds(pl.multiple_of(slice_at * 8, 8), 8), :]
            for g in range(4):
                at = slice(g * GROUP, (g + 1) * GROUP)
                words = m.perm[slice_at, g % 2 * GROUP : (g % 2 + 1) * GROUP, :]
                for level in range(4):
                    value = lax.shift_right_logical(words, g // 2 * 16 + 4 * level) & 15
                    value = value.astype(F32) - 8.0
                    value = value * sc[g : g + 1, level * 128 : (level + 1) * 128]
                    lanes = pl.ds(pl.multiple_of(s * 512 + level * 128, 128), 128)
                    m.wbuf[at, lanes] = value.astype(BF16)
            return carry

        lax.fori_loop(0, 2, dequantize, 0)
        rows = m.xb[...].reshape(256, 512)
        for s in range(2):
            lanes = slice(s * 512, (s + 1) * 512)
            acc = dot(rows, m.wbuf[:, lanes]).astype(BF16)
            acc = dot(acc, m.spread[...]).astype(BF16)
            m.part[r, :, lanes] = acc[0:128]
            m.half_out[r, :, lanes] = acc[128:256]

    def to_sibling(i, src, dst):
        return remote(src, dst, m.sib_s.at[i], m.sib_r.at[i], tensor=sib)

    halves = [to_sibling(r, m.half_out.at[r], m.half_in.at[r]) for r in range(ZH)]
    resid_there = to_sibling(4, m.resid.at[:, other], m.resb.at[c])
    resid_here = to_sibling(4, m.resid.at[:, other], m.resb.at[other])
    gain_there = to_sibling(5, m.gainb.at[c], m.gainb.at[c])
    gain_here = to_sibling(5, m.gainb.at[c], m.gainb.at[other])

    def add_half(r):
        flow.wait(halves[r])
        m.part[r] = (m.part[r].astype(F32) + m.half_in[r].astype(F32)).astype(BF16)

    students = Exchange("fsdp", f, slots(m.stus), slots(m.sb), m.stu_s, m.stu_r)
    value_parts = Exchange("fsdp", f, slots(m.pvs), slots(m.pvr), m.pv_s, m.pv_r)
    targets = [
        Exchange("dp", d, slots(m.osend0), slots(m.trecv0), m.t5a_s, m.t5a_r),
        Exchange("dp", d, slots(m.osend1), slots(m.trecv1), m.t5b_s, m.t5b_r),
    ]
    grads1 = Exchange("fsdp", f, lambda peer: m.g1.at[f], slots(m.g1), m.g1_s, m.g1_r)
    losses = Exchange("fsdp", f, lambda peer: m.lost.at[f], slots(m.lost), m.loss_s, m.loss_r)
    grads2 = Exchange("tensor", t, slots(m.g2s), slots(m.g2r), m.g2_s, m.g2_r)
    grads3 = Exchange("dp", d, lambda peer: m.g3.at[d], slots(m.g3), m.g3_s, m.g3_r)

    def ring(src, name, half):
        relay, near, added, summed, send, recv = (
            getattr(m, f"{name}_{end}") for end in ("relay", "near", "added", "summed", "s", "r")
        )
        low, high = pl.ds(0, half), pl.ds(half, half)
        far = [
            remote(src(2, low), relay.at[0], send.at[0], recv.at[0], tensor=zp),
            remote(src(2, high), relay.at[1], send.at[1], recv.at[1], tensor=zm),
        ]
        direct = [
            remote(src(1, high), near.at[0], send.at[2], recv.at[2], tensor=zp),
            remote(src(3, low), near.at[1], send.at[3], recv.at[3], tensor=zm),
        ]
        sums = [
            remote(added.at[0], summed.at[0], send.at[4], recv.at[4], tensor=zp),
            remote(added.at[1], summed.at[1], send.at[5], recv.at[5], tensor=zm),
        ]
        return far, direct, sums

    far, direct, sums = ring(lambda r, rows: m.part.at[r, rows], "t1", 64)
    partial(2)
    flow.start(halves[2], due=[halves[2]])
    partial(1)
    flow.start(halves[1], due=[halves[1]])
    add_half(2)
    flow.start(*far, due=far)
    flow.wait(from_z)
    flow.start(pass_on(5, fz, fsdp=xp), pass_on(6, fz, fsdp=xm), due=near_other)
    flow.wait(*near_same)
    flow.start(pass_on(3, xm, 0, fsdp=xp), pass_on(4, xp, 1, fsdp=xm), due=far_same)
    partial(3)
    flow.start(halves[3], due=[halves[3]])
    add_half(1)
    flow.start(direct[0], due=direct[:1])
    proj_in.wait()
    partial(0)
    flow.start(halves[0], due=[halves[0]])
    add_half(3)
    flow.start(direct[1], due=direct[1:])
    flow.wait(sent_rows)
    flow.start(value_slices, due=[value_slices])
    share(0, 1, 2, 4)

    resid_in.wait()
    row, col = iotas(512, 512)
    m.resid[...] = dot(m.residt[...], one_hot(row == col), ((0,), (0,))).astype(BF16).reshape(4, 2, 32, 512)
    for b in range(4):
        m.resb[c, b] = m.resid[b, c]
    row, col = iotas(64, 512)
    gain = dot(gain_ref[...], one_hot((col & 63) == row))
    row, col = iotas(8, 512)
    gain = jnp.sum(jnp.where((col >> 6) == row, gain, 0.0), axis=0, keepdims=True)
    m.gainb[c] = jnp.broadcast_to(gain, (8, 512))
    flow.start(resid_there, gain_there, due=[resid_here, gain_here])
    add_half(0)

    flow.wait(*near_other)
    flow.start(pass_on(7, xmz, 0, fsdp=xp), pass_on(8, xpz, 1, fsdp=xm), due=far_other)
    share(5, 6)
    flow.wait(far[0])
    ring_sum(m.t1_added, 0, m.part[1, 0:64], m.t1_relay[0], 1024)
    flow.start(sums[0], due=sums[:1])
    flow.wait(far[1])
    ring_sum(m.t1_added, 1, m.part[3, 64:128], m.t1_relay[1], 1024)
    flow.start(sums[1], due=sums[1:])

    stu_in.wait()
    row, col = iotas(896, 1024)
    pad = one_hot(((col >> 5) * 28 + (col & 31) == row) & ((col & 31) < 28))
    for j in range(2):
        padded = dot(m.stu[:, j * 896 : (j + 1) * 896], pad).astype(BF16)
        for i in range(4):
            m.stus[4 * j + i] = padded[:, i * KVW : (i + 1) * KVW]
    m.sb[f] = m.stus[f]

    places = jnp.broadcast_to(seg_ref[0:1, 0:128].astype(F32), (128, 128))
    same = places == jnp.transpose(places)
    row, col = iotas(128, 128)
    allow = jnp.where(same & (row >= col), 1.0, 0.0)[:LEAD, :LEAD]
    allow = jnp.concatenate([allow] * 7, axis=0)
    q_in.wait()
    k_in.wait()
    for g in range(2):
        heads = [m.q[:, (g * 7 + h) * HEAD : (g * 7 + h + 1) * HEAD] for h in range(7)]
        scores = dot(jnp.concatenate(heads, axis=0), m.k[:, g * HEAD : (g + 1) * HEAD], ((1,), (1,)))
        scores = jnp.where(allow > 0.0, scores * HEAD ** (-0.5), -1e30)
        weights = jnp.exp(scores - jnp.max(scores, axis=1, keepdims=True))
        probs = weights / jnp.sum(weights, axis=1, keepdims=True)
        m.probs[g] = probs.astype(BF16)
        m.probs_t[g] = jnp.transpose(probs).astype(BF16)

    routes_in.wait()
    row, col = iotas(64, 32)
    place = ((d * N + f) * N + t) * 4
    wanted = jnp.full((64, 32), -1, jnp.int32)
    for j in range(4):
        wanted = jnp.where((col >> 3) == j, m.routes[place + j], wanted)
    select = one_hot(((row >> 3) == wanted) & ((row & 7) == (col & 7)))
    lead = lax.broadcasted_iota(jnp.int32, (LEAD, HEAD), 0) >> 3
    mask = jnp.zeros((LEAD, HEAD), F32)
    for source in range(N):
        for j in range(4):
            hit = m.routes[((source * N + f) * N + t) * 4 + j] == d
            mask = jnp.where(lead == source, jnp.maximum(mask, jnp.where(hit, 1.0, 0.0)), mask)

    flow.wait(*far_same)
    share(3)
    flow.wait(*far_other)
    share(7)
    flow.wait(*direct, *sums, resid_here, gain_here)

    lower = m.part[0, 0:64].astype(F32) + m.t1_summed[0].astype(F32) + m.t1_near[1].astype(F32)
    upper = m.part[0, 64:128].astype(F32) + m.t1_near[0].astype(F32) + m.t1_summed[1].astype(F32)
    out = jnp.concatenate([lower, upper], axis=0)
    power = jnp.zeros((128, 1), F32)
    scaled = []
    for s in range(2):
        hidden = out[:, s * 512 : (s + 1) * 512] + m.resb[s].reshape(128, 512).astype(F32)
        power = power + jnp.sum(hidden * hidden, axis=1, keepdims=True)
        scaled.append((hidden * m.gainb[s, 0:1, :]).astype(BF16))
    m.pbuf0[:, :, CHUNKS[0] :] = split_sum(power).reshape(ZH, 32, 128)
    flow.wait(*proj_here)

    def ahead(pbuf):
        return lambda r, rows: pbuf.at[lax.rem(zh + r, ZH), rows]

    rings = [ring(ahead(m.pbuf0), "t4a", 16), ring(ahead(m.pbuf1), "t4b", 16)]
    pbufs = (m.pbuf0, m.pbuf1)
    for i in range(2):
        for j in range(CHUNKS[i] // 256):
            lanes = slice(j * 256, (j + 1) * 256)
            from_lanes = slice(i * CHUNKS[0] + j * 256, i * CHUNKS[0] + (j + 1) * 256)
            acc = jnp.zeros((128, 256), F32)
            for s in range(2):
                rows = [m.proj[s, owner % 2, owner // 2, :, from_lanes] for owner in range(8)]
                acc = acc + dot(scaled[s], jnp.concatenate(rows, axis=0))
            pbufs[i][:, :, lanes] = acc.astype(BF16).reshape(ZH, 32, 256)
        flow.start(*rings[i][0], *rings[i][1], due=rings[i][0] + rings[i][1])
    flow.start(students, due=[students])
    for i, name in enumerate(("t4a", "t4b")):
        far4, direct4, sums4 = rings[i]
        relay, added = getattr(m, f"{name}_relay"), getattr(m, f"{name}_added")
        for way, r in enumerate((1, 3)):
            flow.wait(far4[way])
            mine = pbufs[i][lax.rem(zh + r, ZH), 16 * way : 16 * way + 16]
            ring_sum(added, way, mine, relay[way], CHUNKS[i])
            flow.start(sums4[way], due=[sums4[way]])

    flow.wait(students, value_slices)
    rows_of_value = m.vw[...].reshape(8 * 32, KVW)
    value_part = dot(m.sb[...].reshape(8 * LEAD, KVW), rows_of_value)
    m.pvs[...] = value_part.reshape(8, LEAD, KVW).astype(BF16)
    m.pvr[f] = m.pvs[f]
    m.sb_t[...] = jnp.transpose(m.sb[...].reshape(8 * LEAD, KVW).astype(F32)).astype(BF16)

    row_scale = None
    for i, name in enumerate(("t4a", "t4b")):
        _, direct4, sums4 = rings[i]
        flow.wait(*direct4, *sums4)
        near, summed = getattr(m, f"{name}_near"), getattr(m, f"{name}_summed")
        own = pbufs[i][zh].astype(F32)
        lower = own[0:16] + summed[0].astype(F32) + near[1].astype(F32)
        upper = own[16:32] + near[0].astype(F32) + summed[1].astype(F32)
        total = jnp.concatenate([lower, upper], axis=0)
        if i == 0:
            power = jnp.sum(total[:, CHUNKS[0] :], axis=1, keepdims=True)
            row_scale = lax.rsqrt(power / HT + EPS)
        routed = dot(select, (total[:, : CHUNKS[i]] * row_scale).astype(BF16))
        half = CHUNKS[i] // 2
        osend, trecv = getattr(m, f"osend{i}"), getattr(m, f"trecv{i}")
        osend[...] = jnp.concatenate(
            [routed[:, :half].reshape(8, 8, half), routed[:, half:].reshape(8, 8, half)], axis=1
        ).astype(BF16)
        trecv[d] = osend[d]
        flow.start(targets[i], due=[targets[i]])
    flow.start(value_parts, due=[value_parts])
    flow.wait(value_parts)
    values = m.pvr[0].astype(F32)
    for j in range(1, 8):
        values = values + m.pvr[j].astype(F32)
    values = values.astype(BF16)
    attended = [dot(m.probs[g], values[:, g * HEAD : (g + 1) * HEAD]) for g in range(2)]

    lost = jnp.zeros((LEAD, HEAD), F32)
    pieces_of = ([], [])
    for i in range(2):
        flow.wait(targets[i])
        received = getattr(m, f"trecv{i}")[...].astype(F32)
        per_half = CHUNKS[i] // 2 // HEAD
        for j in range(2 * per_half):
            at, lane = j // per_half * 8, j % per_half * HEAD
            wanted = received[:, at : at + 8, lane : lane + HEAD].reshape(LEAD, HEAD)
            head = i * (CHUNKS[0] // HEAD) + j
            g, h = head // 7, head % 7
            diff = attended[g][h * LEAD : (h + 1) * LEAD] - wanted
            masked = diff * mask
            lost = lost + masked * diff
            pieces_of[g].append((2.0 * masked / QW).astype(BF16))
    for g in range(2):
        grad = dot(m.probs_t[g], jnp.concatenate(pieces_of[g], axis=0))
        m.g1[f, :, g * HEAD : (g + 1) * HEAD] = grad.astype(BF16)
    flow.start(grads1, due=[grads1])
    lost = lost.reshape(8, 8, 128).sum(axis=0)
    m.lost[f] = lost
    flow.start(losses, due=[losses])
    flow.wait(grads1)
    grad = dot(m.sb_t[...], m.g1[...].reshape(8 * LEAD, KVW))
    flow.wait(losses)
    tail = loss_row(jnp.sum(m.lost[...]))
    for j in range(N):
        m.g2s[j] = (grad[32 * j : 32 * j + 32] + tail).astype(BF16)
    m.g2r[t] = m.g2s[t]
    flow.start(grads2, due=[grads2])
    flow.wait(grads2)
    row, _ = iotas(32, KVW)
    total = jnp.sum(m.g2r[...].astype(F32), axis=0)
    m.g3[d] = jnp.where(row < LOSS_ROW, total, loss_row(loss_of(total))).astype(BF16)
    flow.start(grads3, due=[grads3])
    flow.wait(grads3)
    total = jnp.sum(m.g3[...].astype(F32), axis=0)
    grad_ref[...] = total[0:LOSS_ROW]
    loss_ref[0, 0] = loss_of(total) / total_count
    flow.finish()


def local(
    teacher_in,
    codes,
    scales,
    teacher_resid,
    teacher_gain,
    projector,
    routes,
    student_in,
    queries,
    keys,
    segments,
    value_weight,
):
    spec = scratch_spec()
    vmem = pl.BlockSpec(memory_space=pltpu.VMEM)
    smem = pl.BlockSpec(memory_space=pltpu.SMEM)
    hbm = pl.BlockSpec(memory_space=pltpu.HBM)
    loss, grad = pl.pallas_call(
        functools.partial(kernel, float(16384 * QW), tuple(spec)),
        out_shape=(
            jax.ShapeDtypeStruct((1, 1), F32),
            jax.ShapeDtypeStruct((28, KVW), F32),
        ),
        in_specs=[hbm, hbm, vmem, hbm, vmem, hbm, hbm, hbm, vmem, vmem, hbm, hbm],
        out_specs=(smem, vmem),
        scratch_shapes=list(spec.values()),
        compiler_params=pltpu.CompilerParams(
            collective_id=0, has_side_effects=True, vmem_limit_bytes=56 * 1024 * 1024
        ),
        name="distill",
    )(
        teacher_in.reshape(4, 2, 32, 512),
        codes,
        scales,
        teacher_resid.transpose(1, 2, 0).reshape(512, 256),
        teacher_gain,
        projector.reshape(64, QW),
        routes.reshape(2048),
        student_in,
        segments.reshape(1, 256),
        value_weight,
        queries,
        keys,
    )
    return loss[0, 0], grad


def solution(mesh):
    return jax.shard_map(
        local,
        mesh=mesh,
        in_specs=(
            P(("dp", "fsdp"), "tensor"),
            P("tensor", None),
            P("tensor", None),
            P(("dp", "fsdp"), None, "tensor"),
            P(None, "tensor"),
            P("fsdp", "tensor", None),
            P(),
            P(("dp", "fsdp", "tensor"), None),
            P(("dp", "fsdp", "tensor"), None),
            P(("dp", "fsdp", "tensor"), None),
            P(("dp", "fsdp", "tensor")),
            P(("fsdp", "tensor"), None),
        ),
        out_specs=(P(), P(("fsdp", "tensor"), None)),
        check_vma=False,
    )
```
